32 devices in a mesh: dp: 4 (over z), expert: 8 (over y, x, core).
Axes of the slice: x: 2, y: 2, z: 4, core: 2. Of those that a mesh axis runs over, the one named last changes fastest.
Arguments:
- layer_input: bfloat16 [1536, 7168], P('expert', 'dp'), may hold values from -6 to 6
- out_grad: bfloat16 [1536, 7168], P('expert', 'dp'), may hold values from -6 to 6
- routes: int32 [1536, 2], P('expert'), may hold values from 0 to 7, all different within a row; in each aligned block of 192 rows (0 to 191, 192 to 383, ...) at most 96 rows name the same one
- gate_weights: bfloat16 [1536, 2], P('expert'), may hold values from 0.049804688 to 1
- w_gate: bfloat16 [8, 7168, 1024], P('expert', 'dp'), may hold values from -0.0625 to 0.0625
- w_up: bfloat16 [8, 7168, 1024], P('expert', 'dp'), may hold values from -0.0625 to 0.0625
- w_down: bfloat16 [8, 1024, 7168], P('expert', None, 'dp'), may hold values from -0.1875 to 0.1875
Outputs:
- input_grad: bfloat16 [1536, 7168], P('expert', 'dp')
- route_grad: bfloat16 [1536, 2], P('expert')
- grad_gate: bfloat16 [8, 7168, 1024], P('expert', 'dp')
- grad_up: bfloat16 [8, 7168, 1024], P('expert', 'dp')
- grad_down: bfloat16 [8, 1024, 7168], P('expert', None, 'dp')
The draws below stay inside these ranges and needn't reach their ends.
Inputs may be any that keep to these rules, and one draw needn't show every extreme that they name: `routes`: each row names 2 different experts. Among the 192 rows of one index of the expert axis (aligned blocks of rows), no expert is named by more than 96 rows.
All inputs are finite; a program needn't handle non-finite values.
Results may differ from the reference program's by a relative error of at most 0.024.
Values may be sent and summed in bfloat16 or wider, within the bound.
No kernel may reach another device: no remote copies, remote signals or barrier semaphores. Data moves between devices by JAX's collectives and lax.ppermute only.
A program may use at most 128 MiB of HBM per device.

```python
import math
import jax
import jax.numpy as jnp
import numpy as np
from jax import lax

D = 7168
FFW = 1024
KWIN = 2
TOKR = 192
EXPERTS = 8
TOKENS = 1536
CAP = 96
N_DP = 4
N_EXPERT = 8


def block_scale(rng, shape, shards, least, top_value):
    factor_of = 1.0
    for dim, shards_of in shards:
        steps = jax.random.uniform(jax.random.fold_in(jax.random.fold_in(rng, 6), dim), (shards_of,), jnp.float32, least / len(shards), top_value / len(shards))
        factor_of = factor_of * jnp.repeat(jnp.exp(steps), shape[dim] // shards_of).reshape((-1,) + (1,) * (len(shape) - 1 - dim))
    return factor_of


def routed_block(own_key, own, number, rows, number_of, top, bound, slope):
    sequence = jax.random.permutation(own_key, number_of)
    heavy_load, usual = portions_of(number_of, rows * top, bound, slope, True), portions_of(number_of, rows * top, bound, slope, False)
    places = jnp.arange(number_of)

    def named(sizes, offset_by):
        used = int((sizes > 0).sum())
        fixed = max(1, used // 4)
        shifted = fixed + (places - fixed + offset_by * (used - fixed)) % max(1, number_of - fixed)
        return jnp.zeros((number_of,), jnp.int32).at[sequence[jnp.where(places < fixed, places, shifted)]].set(jnp.asarray(sizes, jnp.int32))

    sizes = jnp.where(number % 4 == 0, named(heavy_load, number // 4), named(usual, number - number // 4 - 1))
    mixed = jax.random.permutation(jax.random.fold_in(own, 3), number_of)
    donor, sink = mixed[0:number_of // 2 * 2:2], mixed[1:number_of // 2 * 2:2]
    margin = jnp.minimum(sizes[donor] - 1, bound - sizes[sink]) // 2
    margin = jnp.where((donor == sequence[0]) | (sink == sequence[0]) | (sizes[sink] == 0), 0, jnp.maximum(margin, 0))
    shifted = jax.random.randint(jax.random.fold_in(own, 4), (number_of // 2,), 0, 1 << 20) % (margin + 1)
    sizes = sizes.at[donor].add(-shifted).at[sink].add(shifted)
    labels = jnp.searchsorted(jnp.cumsum(sizes), jnp.arange(rows * top), side="right").astype(jnp.int32)
    grid = labels.reshape(top, rows).T
    grid = grid[jax.random.permutation(jax.random.fold_in(own, 1), rows)]
    offset_by = jax.random.randint(jax.random.fold_in(own, 2), (rows, 1), 0, top)
    return jnp.take_along_axis(grid, (jnp.arange(top)[None, :] + offset_by) % top, axis=1)


def portions_of(amount, total, reach, skew, full):
    loads = [(1 << 20) // math.isqrt(grade ** skew) + 1 for grade in range(1, amount + 1)]
    largest = reach if full else min(reach, max(-(-total // amount), total * loads[0] // sum(loads)))
    least = 1 if total - largest >= amount - 1 else 0
    given, surplus = [largest] + [least] * (amount - 1), total - largest - least * (amount - 1)
    while surplus > 0:
        free = [i for i in range(1, amount) if given[i] < largest] or [i for i in range(1, amount) if given[i] < reach]
        mass, remaining = sum([loads[i] for i in free]), surplus
        for i in free:
            more = min(reach - given[i], max(1, remaining * loads[i] // mass), surplus)
            given[i] = given[i] + more
            surplus = surplus - more
    return np.array(given)


def gaussian(rng, extent, scale, reach, cuts=(), held_as=jnp.bfloat16):
    array = jax.random.normal(rng, extent, jnp.float32) * scale
    if len(cuts) > 0:
        array = block_scale(rng, extent, cuts, -0.22, 0.18) * array
    return jnp.clip(array, min=-reach, max=reach).astype(held_as)


def setup_inputs(seed: int = 0) -> dict:
    keys = jax.random.split(jax.random.key(seed), 8)
    layer_input = gaussian(keys[0], (TOKENS, D), 1.0, 6.0, ((0, 8), (1, 4)))
    out_grad = gaussian(keys[1], (TOKENS, D), 1.0, 6.0, ((0, 8), (1, 4)))
    routes_keys = jax.random.split(jax.random.fold_in(keys[2], 1), TOKENS // TOKR)
    routes_turns = jax.random.permutation(jax.random.fold_in(keys[2], 3), TOKENS // TOKR)
    routes = jax.vmap(lambda own, number: routed_block(jax.random.fold_in(keys[2], 2), own, number, TOKR, EXPERTS, KWIN, CAP, 2))(routes_keys, routes_turns).reshape((TOKENS, KWIN))
    gate_weights = jnp.clip(jnp.exp(math.log(1.0) - 2.9996462 * jax.random.uniform(keys[3], (TOKENS, KWIN), jnp.float32) ** block_scale(keys[3], (TOKENS, KWIN), ((0, 8),), -0.2, 0.2)), 0.049804688, 1.0).astype(jnp.bfloat16)
    w_gate = gaussian(keys[4], (EXPERTS, D, FFW), D ** -0.5, 0.0625, ((0, 8), (1, 4)))
    w_up = gaussian(keys[5], (EXPERTS, D, FFW), D ** -0.5, 0.0625, ((0, 8), (1, 4)))
    w_down = gaussian(keys[6], (EXPERTS, FFW, D), FFW ** -0.5, 0.1875, ((0, 8), (2, 4)))
    return dict(layer_input=layer_input, out_grad=out_grad, routes=routes, gate_weights=gate_weights, w_gate=w_gate, w_up=w_up, w_down=w_down)


def slot_numbers(block_routes, n_experts, capacity):
    flat_routes = block_routes.reshape(-1)
    marked = (flat_routes[:, None] == jnp.arange(n_experts, dtype=jnp.int32)[None, :]).astype(jnp.int32)
    before = jnp.cumsum(marked, axis=0) - marked
    rank_in = jnp.sum(before * marked, axis=1)
    return (flat_routes * capacity + rank_in).astype(jnp.int32)


def slot_owner(slot_row, slot_total):
    route_count = slot_row.shape[0]
    return jnp.zeros((slot_total,), jnp.int32).at[slot_row].set(jnp.arange(1, route_count + 1, dtype=jnp.int32))


def activation_grads(pre_gate, pre_up, back_hidden, weight):
    sigmoid_gate = jax.nn.sigmoid(pre_gate)
    silu_gate = pre_gate * sigmoid_gate
    hidden = silu_gate * pre_up
    route_part = jnp.sum(hidden * back_hidden, axis=1).astype(jnp.bfloat16)
    route_scale = weight.astype(jnp.float32)[:, None]
    scaled_hidden = (route_scale * hidden).astype(jnp.bfloat16)
    gate_pre = (route_scale * back_hidden * pre_up * sigmoid_gate * (1.0 + pre_gate * (1.0 - sigmoid_gate))).astype(jnp.bfloat16)
    up_pre = (route_scale * back_hidden * silu_gate).astype(jnp.bfloat16)
    return scaled_hidden, gate_pre, up_pre, route_part


def blocked(partials):
    rounded = lax.optimization_barrier(partials.astype(jnp.bfloat16))
    return jnp.sum(rounded.astype(jnp.float32), axis=0)


def reference(layer_input, out_grad, routes, gate_weights, w_gate, w_up, w_down):
    width_block = D // N_DP
    slot_total = N_EXPERT * CAP
    blocks = routes.reshape(N_EXPERT, TOKR * KWIN)
    slot_table = jax.vmap(lambda block_row: slot_numbers(block_row, EXPERTS, CAP))(blocks)
    owners = jax.vmap(lambda slot_row: slot_owner(slot_row, EXPERTS * CAP))(slot_table)
    flat_gates = gate_weights.reshape(-1)
    block_base = jnp.arange(N_EXPERT, dtype=jnp.int32)[:, None] * (TOKR * KWIN)

    def per_expert(carried, expert):
        carry_grad, carry_route = carried
        owner_part = lax.dynamic_slice_in_dim(owners, expert * CAP, CAP, 1)
        valid_slot = (owner_part > 0).reshape(-1)
        local_route = jnp.maximum(owner_part - 1, 0)
        route_index = (block_base + local_route).reshape(-1).astype(jnp.int32)
        token_index = (route_index // KWIN).astype(jnp.int32)
        zero_value = jnp.zeros((), jnp.bfloat16)
        rows_in = jnp.where(valid_slot[:, None], layer_input[token_index], zero_value)
        rows_grad = jnp.where(valid_slot[:, None], out_grad[token_index], zero_value)
        weight = jnp.where(valid_slot, flat_gates[route_index], zero_value)
        gate_mat = lax.dynamic_index_in_dim(w_gate, expert, 0, keepdims=False).astype(jnp.float32)
        up_mat = lax.dynamic_index_in_dim(w_up, expert, 0, keepdims=False).astype(jnp.float32)
        down_mat = lax.dynamic_index_in_dim(w_down, expert, 0, keepdims=False).astype(jnp.float32)
        wide_in = rows_in.astype(jnp.float32).reshape(slot_total, N_DP, width_block)
        wide_grad = rows_grad.astype(jnp.float32).reshape(slot_total, N_DP, width_block)
        pre_gate = blocked(jnp.einsum("snd,ndf->nsf", wide_in, gate_mat.reshape(N_DP, width_block, FFW)))
        pre_up = blocked(jnp.einsum("snd,ndf->nsf", wide_in, up_mat.reshape(N_DP, width_block, FFW)))
        back_hidden = blocked(jnp.einsum("snd,fnd->nsf", wide_grad, down_mat.reshape(FFW, N_DP, width_block)))
        scaled_hidden, gate_pre, up_pre, route_part = activation_grads(pre_gate, pre_up, back_hidden, weight)
        rows_in32 = rows_in.astype(jnp.float32)
        gate_pre32 = gate_pre.astype(jnp.float32)
        up_pre32 = up_pre.astype(jnp.float32)
        grad_down_one = jnp.einsum("sf,sd->fd", scaled_hidden.astype(jnp.float32), rows_grad.astype(jnp.float32)).astype(jnp.bfloat16)
        grad_gate_one = jnp.einsum("sd,sf->df", rows_in32, gate_pre32).astype(jnp.bfloat16)
        grad_up_one = jnp.einsum("sd,sf->df", rows_in32, up_pre32).astype(jnp.bfloat16)
        slot_grad = (jnp.einsum("sf,df->sd", gate_pre32, gate_mat) + jnp.einsum("sf,df->sd", up_pre32, up_mat)).astype(jnp.bfloat16)
        target = jnp.where(valid_slot, route_index, TOKENS * KWIN).astype(jnp.int32)
        carry_grad = carry_grad.at[target].set(slot_grad, mode="drop")
        carry_route = carry_route.at[target].set(route_part, mode="drop")
        return (carry_grad, carry_route), (grad_gate_one, grad_up_one, grad_down_one)

    start = (jnp.zeros((TOKENS * KWIN, D), jnp.bfloat16), jnp.zeros((TOKENS * KWIN,), jnp.bfloat16))
    (route_rows, route_values), stacked = lax.scan(per_expert, start, jnp.arange(EXPERTS, dtype=jnp.int32))
    grad_gate, grad_up, grad_down = stacked
    input_grad = jnp.sum(route_rows.reshape(TOKENS, KWIN, D).astype(jnp.float32), axis=1).astype(jnp.bfloat16)
    route_grad = route_values.reshape(TOKENS, KWIN)
    return input_grad, route_grad, grad_gate, grad_up, grad_down
```

```python
import jax
import jax.numpy as jnp
from jax import lax
from jax.sharding import PartitionSpec as P

BF16 = jnp.bfloat16
F32 = jnp.float32


def line_sum(part, axis, size, place):
    half = size // 2
    total = part
    for k in range(half - 1):
        pairs = [(k, k + 1), (size - 1 - k, size - 2 - k)]
        arrived = lax.ppermute(total, axis, pairs)
        total = (total.astype(F32) + arrived.astype(F32)).astype(BF16)
    arrived = lax.ppermute(total, axis, [(half - 1, half), (half, half - 1)])
    total = (total.astype(F32) + arrived.astype(F32)).astype(BF16)
    depth = jnp.where(place < half, half - 1 - place, place - half)
    for k in range(half - 1):
        pairs = [(half - 1 - k, half - 2 - k), (half + k, half + k + 1)]
        arrived = lax.ppermute(total, axis, pairs)
        total = jnp.where(depth == k + 1, arrived, total)
    return total


def activation_grads(sums, weight, units):
    pre_gate = sums[:, :units].astype(F32)
    pre_up = sums[:, units : 2 * units].astype(F32)
    back_hidden = sums[:, 2 * units :].astype(F32)
    sigmoid_gate = jax.nn.sigmoid(pre_gate)
    silu_gate = pre_gate * sigmoid_gate
    hidden = silu_gate * pre_up
    route_part = jnp.sum(hidden * back_hidden, axis=1, keepdims=True).astype(BF16)
    scale = weight.astype(F32)
    scaled_hidden = (scale * hidden).astype(BF16)
    gate_pre = (
        scale * back_hidden * pre_up * sigmoid_gate * (1.0 + pre_gate * (1.0 - sigmoid_gate))
    ).astype(BF16)
    up_pre = (scale * back_hidden * silu_gate).astype(BF16)
    return (scaled_hidden, gate_pre, up_pre, route_part)


def body(layer_input, out_grad, routes, gate_weights, w_gate, w_up, w_down):
    groups = lax.axis_size("expert")
    n_dp = lax.axis_size("dp")
    me = lax.axis_index("expert")
    place = lax.axis_index("dp")
    tokens, width = layer_input.shape
    choose = routes.shape[1]
    units = w_gate.shape[2]
    capacity = 2 * tokens * choose // groups
    per_chunk = max(1, groups // 8)
    offsets = sorted(range(groups), key=lambda r: (bin(r >> 1).count("1"), r))
    chunks = [offsets[i : i + per_chunk] for i in range(0, groups, per_chunk)]

    partner = me ^ jnp.arange(groups, dtype=jnp.int32)
    named = routes[:, :, None] == partner[None, None, :]
    chosen = jnp.any(named, axis=1)
    rank = jnp.cumsum(chosen.astype(jnp.int32), axis=0) - 1
    rank = jnp.where(chosen, rank, -1).T
    slot = jnp.arange(capacity, dtype=jnp.int32)
    pick = (rank[:, None, :] == slot[None, :, None]).astype(BF16)

    lanes = 128
    extra = jnp.concatenate([gate_weights, routes[:, :1].astype(BF16)], axis=1)
    extra = jnp.pad(extra, ((0, 0), (0, lanes - choose - 1)))
    packed = jnp.concatenate([layer_input, out_grad, extra], axis=1)

    gate_mat, up_mat, down_mat = w_gate[0], w_up[0], w_down[0]
    over_units = (((1,), (1,)), ((), ()))
    over_rows = (((0,), (0,)), ((), ()))

    got = {}
    for r in offsets:
        rows = jnp.dot(pick[r], packed, preferred_element_type=F32).astype(BF16)
        if r:
            rows = lax.ppermute(rows, "expert", [(i, i ^ r) for i in range(groups)])
        got[r] = rows

    kept = []
    returned = {}
    for chunk in chunks:
        rows = [got[r] for r in chunk]
        rows = rows[0] if len(rows) == 1 else jnp.concatenate(rows, axis=0)
        rows_in = rows[:, :width]
        rows_grad = rows[:, width : 2 * width]
        tail = rows[:, 2 * width :]
        weight = jnp.where(tail[:, 2:3] == me.astype(BF16), tail[:, 0:1], tail[:, 1:2])
        part_gate = jnp.dot(rows_in, gate_mat, preferred_element_type=F32)
        part_up = jnp.dot(rows_in, up_mat, preferred_element_type=F32)
        part_back = lax.dot_general(rows_grad, down_mat, over_units, preferred_element_type=F32)
        part = jnp.concatenate(
            [part_gate.astype(BF16), part_up.astype(BF16), part_back.astype(BF16)], axis=1
        )
        sums = line_sum(part, "dp", n_dp, place)
        scaled_hidden, gate_pre, up_pre, route_part = activation_grads(sums, weight, units)
        slot_grad = (
            lax.dot_general(gate_pre, gate_mat, over_units, preferred_element_type=F32)
            + lax.dot_general(up_pre, up_mat, over_units, preferred_element_type=F32)
        ).astype(BF16)
        back = jnp.concatenate(
            [slot_grad, jnp.broadcast_to(route_part, (route_part.shape[0], lanes))], axis=1
        )
        kept.append((rows_in, rows_grad, scaled_hidden, gate_pre, up_pre))
        for i, r in enumerate(chunk):
            one = back[i * capacity : (i + 1) * capacity]
            if r:
                one = lax.ppermute(one, "expert", [(i, i ^ r) for i in range(groups)])
            returned[r] = one

    all_in, all_grad, all_hidden, all_gate, all_up = (
        jnp.concatenate([k[i] for k in kept], axis=0) for i in range(5)
    )
    grad_down = lax.dot_general(all_hidden, all_grad, over_rows, preferred_element_type=F32)
    grad_gate = lax.dot_general(all_in, all_gate, over_rows, preferred_element_type=F32)
    grad_up = lax.dot_general(all_in, all_up, over_rows, preferred_element_type=F32)

    back_all = jnp.concatenate([returned[r] for r in range(groups)], axis=0)
    spread = pick.reshape(groups * capacity, tokens)
    input_grad = lax.dot_general(
        spread, back_all[:, :width], over_rows, preferred_element_type=F32
    ).astype(BF16)
    route_cols = back_all[:, width].reshape(groups, capacity)
    per_offset = jnp.einsum(
        "rst,rs->tr", pick, route_cols, preferred_element_type=F32
    )
    route_grad = jnp.sum(jnp.where(named, per_offset[:, None, :], 0.0), axis=2).astype(BF16)
    return (
        input_grad,
        route_grad,
        grad_gate.astype(BF16)[None],
        grad_up.astype(BF16)[None],
        grad_down.astype(BF16)[None],
    )


def solution(mesh):
    placed = (
        P("expert", "dp"),
        P("expert", "dp"),
        P("expert", None),
        P("expert", None),
        P("expert", "dp", None),
        P("expert", "dp", None),
        P("expert", None, "dp"),
    )
    return jax.shard_map(
        body,
        mesh=mesh,
        in_specs=placed,
        out_specs=(
            P("expert", "dp"),
            P("expert", None),
            P("expert", "dp", None),
            P("expert", "dp", None),
            P("expert", None, "dp"),
        ),
        check_vma=False,
    )
```

```python
import jax
import jax.numpy as jnp
from jax import lax
from jax.sharding import PartitionSpec as P

BF16 = jnp.bfloat16
F32 = jnp.float32


def line_sum(part, axis, size, place):
    half = size // 2
    total = part
    for k in range(half - 1):
        pairs = [(k, k + 1), (size - 1 - k, size - 2 - k)]
        arrived = lax.ppermute(total, axis, pairs)
        total = (total.astype(F32) + arrived.astype(F32)).astype(BF16)
    arrived = lax.ppermute(total, axis, [(half - 1, half), (half, half - 1)])
    total = (total.astype(F32) + arrived.astype(F32)).astype(BF16)
    depth = jnp.where(place < half, half - 1 - place, place - half)
    for k in range(half - 1):
        pairs = [(half - 1 - k, half - 2 - k), (half + k, half + k + 1)]
        arrived = lax.ppermute(total, axis, pairs)
        total = jnp.where(depth == k + 1, arrived, total)
    return total


def activation_grads(sums, weight, units):
    pre_gate = sums[:, :units].astype(F32)
    pre_up = sums[:, units : 2 * units].astype(F32)
    back_hidden = sums[:, 2 * units :].astype(F32)
    sigmoid_gate = jax.nn.sigmoid(pre_gate)
    silu_gate = pre_gate * sigmoid_gate
    hidden = silu_gate * pre_up
    route_part = jnp.sum(hidden * back_hidden, axis=1, keepdims=True).astype(BF16)
    scale = weight.astype(F32)
    scaled_hidden = (scale * hidden).astype(BF16)
    gate_pre = (
        scale * back_hidden * pre_up * sigmoid_gate * (1.0 + pre_gate * (1.0 - sigmoid_gate))
    ).astype(BF16)
    up_pre = (scale * back_hidden * silu_gate).astype(BF16)
    return (scaled_hidden, gate_pre, up_pre, route_part)


def body(layer_input, out_grad, routes, gate_weights, w_gate, w_up, w_down):
    groups = lax.axis_size("expert")
    n_dp = lax.axis_size("dp")
    me = lax.axis_index("expert")
    place = lax.axis_index("dp")
    tokens, width = layer_input.shape
    choose = routes.shape[1]
    units = w_gate.shape[2]
    capacity = 2 * tokens * choose // groups
    per_chunk = max(1, groups // 8)
    offsets = sorted(range(groups), key=lambda r: (bin(r >> 1).count("1"), r))
    chunks = [offsets[i : i + per_chunk] for i in range(0, groups, per_chunk)]

    partner = me ^ jnp.arange(groups, dtype=jnp.int32)
    named = routes[:, :, None] == partner[None, None, :]
    chosen = jnp.any(named, axis=1)
    rank = jnp.cumsum(chosen.astype(jnp.int32), axis=0) - 1
    rank = jnp.where(chosen, rank, -1).T
    slot = jnp.arange(capacity, dtype=jnp.int32)
    pick = (rank[:, None, :] == slot[None, :, None]).astype(BF16)

    lanes = 128
    extra = jnp.concatenate([gate_weights, routes[:, :1].astype(BF16)], axis=1)
    extra = jnp.pad(extra, ((0, 0), (0, lanes - choose - 1)))
    packed = jnp.concatenate([layer_input, out_grad, extra], axis=1)

    gate_mat, up_mat, down_mat = w_gate[0], w_up[0], w_down[0]
    over_units = (((1,), (1,)), ((), ()))
    over_rows = (((0,), (0,)), ((), ()))

    middle = (place == n_dp // 2 - 1) | (place == n_dp // 2)

    def after(value, earlier):
        if earlier is None:
            return value
        return lax.optimization_barrier((value, earlier))[0]

    def fetch(chunk, earlier):
        fetched = []
        for r in chunk:
            rows = jnp.dot(after(pick[r], earlier), packed, preferred_element_type=F32).astype(BF16)
            if r:
                rows = lax.ppermute(rows, "expert", [(i, i ^ r) for i in range(groups)])
            fetched.append(rows)
        return fetched[0] if len(fetched) == 1 else jnp.concatenate(fetched, axis=0)

    def forward(rows):
        rows_in = rows[:, :width]
        rows_grad = rows[:, width : 2 * width]
        part_gate = jnp.dot(rows_in, gate_mat, preferred_element_type=F32)
        part_up = jnp.dot(rows_in, up_mat, preferred_element_type=F32)
        part_back = lax.dot_general(rows_grad, down_mat, over_units, preferred_element_type=F32)
        return jnp.concatenate(
            [part_gate.astype(BF16), part_up.astype(BF16), part_back.astype(BF16)], axis=1
        )

    kept = {}
    returned = {}

    def backward(number, rows, sums):
        chunk = chunks[number]
        tail = rows[:, 2 * width :]
        weight = jnp.where(tail[:, 2:3] == me.astype(BF16), tail[:, 0:1], tail[:, 1:2])
        scaled_hidden, gate_pre, up_pre, route_part = activation_grads(sums, weight, units)
        slot_grad = (
            lax.dot_general(gate_pre, gate_mat, over_units, preferred_element_type=F32)
            + lax.dot_general(up_pre, up_mat, over_units, preferred_element_type=F32)
        ).astype(BF16)
        back = jnp.concatenate(
            [slot_grad, jnp.broadcast_to(route_part, (route_part.shape[0], lanes))], axis=1
        )
        kept[number] = (
            rows[:, :width],
            rows[:, width : 2 * width],
            scaled_hidden,
            gate_pre,
            up_pre,
        )
        for i, r in enumerate(chunk):
            one = back[i * capacity : (i + 1) * capacity]
            if r:
                one = lax.ppermute(one, "expert", [(i, i ^ r) for i in range(groups)])
            returned[r] = one

    count = len(chunks)
    held = {}
    parts = {}
    if n_dp != 4:
        for c in range(count):
            rows = fetch(chunks[c], None)
            backward(c, rows, line_sum(forward(rows), "dp", n_dp, place))
    else:
        inward, across, outward = [(0, 1), (3, 2)], [(1, 2), (2, 1)], [(1, 0), (2, 3)]
        moved, partly, total = {}, {}, {}
        for c in range(min(4, count)):
            held[c] = fetch(chunks[c], None)
        parts[0] = forward(held[0])
        for s in range(count + 2):
            if s >= count:
                sent, pairs = total[s - 2], outward
            elif s < 2:
                sent, pairs = parts[s], inward
            else:
                sent, pairs = jnp.where(middle, total[s - 2], parts[s]), inward + outward
            moved[s] = lax.ppermute(sent, "dp", pairs)
            if 1 <= s <= count:
                crossed = lax.ppermute(partly[s - 1], "dp", across)
                total[s - 1] = (partly[s - 1].astype(F32) + crossed.astype(F32)).astype(BF16)
            if s + 4 < count:
                held[s + 4] = fetch(chunks[s + 4], moved[s])
            if s + 1 < count:
                parts[s + 1] = forward(after(held[s + 1], moved.get(s - 1)))
            if s < count:
                partly[s] = (parts[s].astype(F32) + moved[s].astype(F32)).astype(BF16)
            if s >= 2:
                backward(s - 2, held[s - 2], jnp.where(middle, total[s - 2], moved[s]))
    kept = [kept[c] for c in range(count)]

    all_in, all_grad, all_hidden, all_gate, all_up = (
        jnp.concatenate([k[i] for k in kept], axis=0) for i in range(5)
    )
    grad_down = lax.dot_general(all_hidden, all_grad, over_rows, preferred_element_type=F32)
    grad_gate = lax.dot_general(all_in, all_gate, over_rows, preferred_element_type=F32)
    grad_up = lax.dot_general(all_in, all_up, over_rows, preferred_element_type=F32)

    back_all = jnp.concatenate([returned[r] for r in range(groups)], axis=0)
    spread = pick.reshape(groups * capacity, tokens)
    input_grad = lax.dot_general(
        spread, back_all[:, :width], over_rows, preferred_element_type=F32
    ).astype(BF16)
    route_cols = back_all[:, width].reshape(groups, capacity)
    per_offset = jnp.einsum(
        "rst,rs->tr", pick, route_cols, preferred_element_type=F32
    )
    route_grad = jnp.sum(jnp.where(named, per_offset[:, None, :], 0.0), axis=2).astype(BF16)
    return (
        input_grad,
        route_grad,
        grad_gate.astype(BF16)[None],
        grad_up.astype(BF16)[None],
        grad_down.astype(BF16)[None],
    )


def solution(mesh):
    placed = (
        P("expert", "dp"),
        P("expert", "dp"),
        P("expert", None),
        P("expert", None),
        P("expert", "dp", None),
        P("expert", "dp", None),
        P("expert", None, "dp"),
    )
    return jax.shard_map(
        body,
        mesh=mesh,
        in_specs=placed,
        out_specs=(
            P("expert", "dp"),
            P("expert", None),
            P("expert", "dp", None),
            P("expert", "dp", None),
            P("expert", None, "dp"),
        ),
        check_vma=False,
    )
```

```python
import jax
import jax.numpy as jnp
from jax import lax
from jax.sharding import PartitionSpec as P

BF16 = jnp.bfloat16
F32 = jnp.float32


def line_sum(part, axis, size, place):
    half = size // 2
    total = part
    for k in range(half - 1):
        pairs = [(k, k + 1), (size - 1 - k, size - 2 - k)]
        arrived = lax.ppermute(total, axis, pairs)
        total = (total.astype(F32) + arrived.astype(F32)).astype(BF16)
    arrived = lax.ppermute(total, axis, [(half - 1, half), (half, half - 1)])
    total = (total.astype(F32) + arrived.astype(F32)).astype(BF16)
    depth = jnp.where(place < half, half - 1 - place, place - half)
    for k in range(half - 1):
        pairs = [(half - 1 - k, half - 2 - k), (half + k, half + k + 1)]
        arrived = lax.ppermute(total, axis, pairs)
        total = jnp.where(depth == k + 1, arrived, total)
    return total


def activation_grads(sums, weight):
    pre_gate, pre_up, back_hidden = (one.astype(F32) for one in sums)
    sigmoid_gate = jax.nn.sigmoid(pre_gate)
    silu_gate = pre_gate * sigmoid_gate
    hidden = silu_gate * pre_up
    route_part = jnp.sum(hidden * back_hidden, axis=1, keepdims=True).astype(BF16)
    scale = weight.astype(F32)
    scaled_hidden = (scale * hidden).astype(BF16)
    gate_pre = (
        scale * back_hidden * pre_up * sigmoid_gate * (1.0 + pre_gate * (1.0 - sigmoid_gate))
    ).astype(BF16)
    up_pre = (scale * back_hidden * silu_gate).astype(BF16)
    return (scaled_hidden, gate_pre, up_pre, route_part)


def body(layer_input, out_grad, routes, gate_weights, w_gate, w_up, w_down):
    groups = lax.axis_size("expert")
    n_dp = lax.axis_size("dp")
    me = lax.axis_index("expert")
    place = lax.axis_index("dp")
    tokens, width = layer_input.shape
    choose = routes.shape[1]
    capacity = 2 * tokens * choose // groups
    per_chunk = max(1, groups // 4)
    offsets = [0, 1, 3, 5, 6, 7, 2, 4] if groups == 8 else list(range(groups))
    chunks = [offsets[i : i + per_chunk] for i in range(0, groups, per_chunk)]

    partner = me ^ jnp.arange(groups, dtype=jnp.int32)
    named = routes[:, :, None] == partner[None, None, :]
    chosen = jnp.any(named, axis=1)
    rank = jnp.cumsum(chosen.astype(jnp.int32), axis=0) - 1
    rank = jnp.where(chosen, rank, -1).T
    slot = jnp.arange(capacity, dtype=jnp.int32)
    pick = (rank[:, None, :] == slot[None, :, None]).astype(BF16)

    lanes = 128
    extra = jnp.concatenate([gate_weights, routes[:, :1].astype(BF16)], axis=1)
    extra = jnp.pad(extra, ((0, 0), (0, lanes - choose - 1)))
    packed = jnp.concatenate([layer_input, out_grad, extra], axis=1)

    gate_mat, up_mat, down_mat = w_gate[0], w_up[0], w_down[0]
    over_units = (((1,), (1,)), ((), ()))
    over_rows = (((0,), (0,)), ((), ()))

    middle = (place == n_dp // 2 - 1) | (place == n_dp // 2)

    last = [None]

    def gate(*values):
        if last[0] is None:
            return values
        return lax.optimization_barrier((*values, last[0]))[:-1]

    def mark(value):
        last[0] = value
        return value

    def fetch(r):
        (one,) = gate(pick[r])
        rows = jnp.dot(one, packed, preferred_element_type=F32).astype(BF16)
        mark(rows)
        if r:
            rows = lax.ppermute(rows, "expert", [(i, i ^ r) for i in range(groups)])
        return rows

    def join(rows):
        rows = gate(*rows)
        return rows[0] if len(rows) == 1 else jnp.concatenate(rows, axis=0)

    def forward(rows, which):
        if which == 2:
            part = lax.dot_general(
                rows[:, width : 2 * width], down_mat, over_units, preferred_element_type=F32
            )
        else:
            part = jnp.dot(
                rows[:, :width], (gate_mat, up_mat)[which], preferred_element_type=F32
            )
        return part.astype(BF16)

    count = len(chunks)
    pieces = 3 * count
    kept = {}
    held = {}
    returned = {}

    def activate(c, sums):
        tail = held[c][:, 2 * width :]
        weight = jnp.where(tail[:, 2:3] == me.astype(BF16), tail[:, 0:1], tail[:, 1:2])
        scaled_hidden, gate_pre, up_pre, route_part = activation_grads(sums, weight)
        kept[c] = [
            held[c][:, :width],
            held[c][:, width : 2 * width],
            scaled_hidden,
            gate_pre,
            up_pre,
            route_part,
        ]
        mark(up_pre)

    def to_input(c):
        gate_pre, up_pre = gate(*kept[c][3:5])
        slot_grad = (
            lax.dot_general(gate_pre, gate_mat, over_units, preferred_element_type=F32)
            + lax.dot_general(up_pre, up_mat, over_units, preferred_element_type=F32)
        ).astype(BF16)
        kept[c].append(mark(slot_grad))

    def give_back(c):
        route_part, slot_grad = gate(*kept[c][5:])
        back = jnp.concatenate(
            [slot_grad, jnp.broadcast_to(route_part, (route_part.shape[0], lanes))], axis=1
        )
        for i, r in enumerate(chunks[c]):
            one = back[i * capacity : (i + 1) * capacity]
            mark(one)
            if r:
                one = lax.ppermute(one, "expert", [(i, i ^ r) for i in range(groups)])
            returned[r] = one

    if n_dp != 4:
        for c in range(count):
            held[c] = join([fetch(r) for r in chunks[c]])
            activate(c, [line_sum(forward(held[c], a), "dp", n_dp, place) for a in range(3)])
            to_input(c)
            give_back(c)
    else:
        inward, across, outward = [(0, 1), (3, 2)], [(1, 2), (2, 1)], [(1, 0), (2, 3)]
        part, partly, total = {}, {}, {}
        arrived, crossed, spread_out = {}, {}, {}
        rows = {r: fetch(r) for r in reversed(chunks[0])}
        to_fetch = offsets[len(chunks[0]) :]
        to_do = []

        def send_part(k):
            c, which = divmod(k, 3)
            if which == 0:
                held[c] = join([rows[r] for r in chunks[c]])
                (source,) = (held[c],)
            else:
                (source,) = gate(held[c])
            part[k] = mark(forward(source, which))
            arrived[k] = lax.ppermute(part[k], "dp", inward)

        send_part(0)
        for t in range(pieces + 3):
            if 1 <= t <= pieces:
                k = t - 1
                (came,) = gate(arrived[k])
                partly[k] = mark((part[k].astype(F32) + came.astype(F32)).astype(BF16))
                crossed[k] = lax.ppermute(partly[k], "dp", across)
            if t + 1 < pieces:
                send_part(t + 1)
            if 2 <= t <= pieces + 1:
                k = t - 2
                (came,) = gate(crossed[k])
                total[k] = mark((partly[k].astype(F32) + came.astype(F32)).astype(BF16))
                spread_out[k] = lax.ppermute(total[k], "dp", outward)
            for r in to_fetch[:per_chunk]:
                rows[r] = fetch(r)
            to_fetch = to_fetch[per_chunk:]
            if t >= 5 and t % 3 == 2:
                c = (t - 5) // 3
                to_do += [(activate, c), (to_input, c), (give_back, c)]
            if to_do:
                step, c = to_do.pop(0)
                if step is activate:
                    came = gate(*[spread_out[3 * c + a] for a in range(3)])
                    activate(c, [jnp.where(middle, total[3 * c + a], came[a]) for a in range(3)])
                else:
                    step(c)
        for step, c in to_do:
            step(c)
    kept = [kept[c] for c in range(count)]
    for c in range(count - 1):
        for r, one in zip(chunks[c], gate(*[returned[r] for r in chunks[c]])):
            returned[r] = one

    all_in, all_grad, all_hidden, all_gate, all_up = (
        jnp.concatenate([k[i] for k in kept], axis=0) for i in range(5)
    )
    grad_down = lax.dot_general(all_hidden, all_grad, over_rows, preferred_element_type=F32)
    grad_gate = lax.dot_general(all_in, all_gate, over_rows, preferred_element_type=F32)
    grad_up = lax.dot_general(all_in, all_up, over_rows, preferred_element_type=F32)
    grad_down, grad_gate, grad_up = (g.astype(BF16) for g in (grad_down, grad_gate, grad_up))
    final = chunks[-1]
    for r, one in zip(
        final,
        lax.optimization_barrier(
            (*[returned[r] for r in final], *[g[:8, :128] for g in (grad_down, grad_gate, grad_up)])
        ),
    ):
        returned[r] = one

    back_all = jnp.concatenate([returned[r] for r in range(groups)], axis=0)
    spread = pick.reshape(groups * capacity, tokens)
    input_grad = lax.dot_general(
        spread, back_all[:, :width], over_rows, preferred_element_type=F32
    ).astype(BF16)
    route_cols = back_all[:, width].reshape(groups, capacity)
    per_offset = jnp.einsum(
        "rst,rs->tr", pick, route_cols, preferred_element_type=F32
    )
    route_grad = jnp.sum(jnp.where(named, per_offset[:, None, :], 0.0), axis=2).astype(BF16)
    return (
        input_grad,
        route_grad,
        grad_gate[None],
        grad_up[None],
        grad_down[None],
    )


def solution(mesh):
    placed = (
        P("expert", "dp"),
        P("expert", "dp"),
        P("expert", None),
        P("expert", None),
        P("expert", "dp", None),
        P("expert", "dp", None),
        P("expert", None, "dp"),
    )
    return jax.shard_map(
        body,
        mesh=mesh,
        in_specs=placed,
        out_specs=(
            P("expert", "dp"),
            P("expert", None),
            P("expert", "dp", None),
            P("expert", "dp", None),
            P("expert", None, "dp"),
        ),
        check_vma=False,
    )
```

```python
import jax
import jax.numpy as jnp
from jax import lax
from jax.sharding import PartitionSpec as P

BF16 = jnp.bfloat16
F32 = jnp.float32


def line_sum(part, axis, size, place):
    half = size // 2
    total = part
    for k in range(half - 1):
        pairs = [(k, k + 1), (size - 1 - k, size - 2 - k)]
        arrived = lax.ppermute(total, axis, pairs)
        total = (total.astype(F32) + arrived.astype(F32)).astype(BF16)
    arrived = lax.ppermute(total, axis, [(half - 1, half), (half, half - 1)])
    total = (total.astype(F32) + arrived.astype(F32)).astype(BF16)
    depth = jnp.where(place < half, half - 1 - place, place - half)
    for k in range(half - 1):
        pairs = [(half - 1 - k, half - 2 - k), (half + k, half + k + 1)]
        arrived = lax.ppermute(total, axis, pairs)
        total = jnp.where(depth == k + 1, arrived, total)
    return total


def activation_grads(sums, weight):
    pre_gate, pre_up, back_hidden = (one.astype(F32) for one in sums)
    sigmoid_gate = jax.nn.sigmoid(pre_gate)
    silu_gate = pre_gate * sigmoid_gate
    hidden = silu_gate * pre_up
    route_part = jnp.sum(hidden * back_hidden, axis=1, keepdims=True).astype(BF16)
    scale = weight.astype(F32)
    scaled_hidden = (scale * hidden).astype(BF16)
    gate_pre = (
        scale * back_hidden * pre_up * sigmoid_gate * (1.0 + pre_gate * (1.0 - sigmoid_gate))
    ).astype(BF16)
    up_pre = (scale * back_hidden * silu_gate).astype(BF16)
    return (scaled_hidden, gate_pre, up_pre, route_part)


def body(layer_input, out_grad, routes, gate_weights, w_gate, w_up, w_down):
    groups = lax.axis_size("expert")
    n_dp = lax.axis_size("dp")
    me = lax.axis_index("expert")
    place = lax.axis_index("dp")
    tokens, width = layer_input.shape
    choose = routes.shape[1]
    capacity = 2 * tokens * choose // groups
    per_chunk = max(1, groups // 4)
    offsets = [0, 1, 3, 5, 2, 4, 6, 7] if groups == 8 else list(range(groups))
    chunks = [offsets[i : i + per_chunk] for i in range(0, groups, per_chunk)]

    partner = me ^ jnp.arange(groups, dtype=jnp.int32)
    named = routes[:, :, None] == partner[None, None, :]
    chosen = jnp.any(named, axis=1)
    rank = jnp.cumsum(chosen.astype(jnp.int32), axis=0) - 1
    rank = jnp.where(chosen, rank, -1).T
    slot = jnp.arange(capacity, dtype=jnp.int32)
    pick = (rank[:, None, :] == slot[None, :, None]).astype(BF16)

    lanes = 128
    extra = jnp.concatenate([gate_weights, routes[:, :1].astype(BF16)], axis=1)
    extra = jnp.pad(extra, ((0, 0), (0, lanes - choose - 1)))
    packed = jnp.concatenate([layer_input, out_grad, extra], axis=1)

    gate_mat, up_mat, down_mat = w_gate[0], w_up[0], w_down[0]
    over_units = (((1,), (1,)), ((), ()))
    over_rows = (((0,), (0,)), ((), ()))

    middle = (place == n_dp // 2 - 1) | (place == n_dp // 2)

    last = [None]

    def gate(*values):
        if last[0] is None:
            return values
        return lax.optimization_barrier((*values, last[0]))[:-1]

    def mark(value):
        last[0] = value
        return value

    def fetch(r):
        (one,) = gate(pick[r])
        rows = jnp.dot(one, packed, preferred_element_type=F32).astype(BF16)
        mark(rows)
        if r:
            rows = lax.ppermute(rows, "expert", [(i, i ^ r) for i in range(groups)])
        return rows

    def join(rows):
        rows = gate(*rows)
        return rows[0] if len(rows) == 1 else jnp.concatenate(rows, axis=0)

    halves = 2
    part_units = w_gate.shape[2] // halves

    def forward(rows, half):
        cols = slice(half * part_units, (half + 1) * part_units)
        rows_in, rows_grad = rows[:, :width], rows[:, width : 2 * width]
        part_gate = jnp.dot(rows_in, gate_mat[:, cols], preferred_element_type=F32)
        part_up = jnp.dot(rows_in, up_mat[:, cols], preferred_element_type=F32)
        part_back = lax.dot_general(
            rows_grad, down_mat[cols], over_units, preferred_element_type=F32
        )
        return jnp.concatenate(
            [part_gate.astype(BF16), part_up.astype(BF16), part_back.astype(BF16)], axis=1
        )

    count = len(chunks)
    pieces = halves * count
    kept = {}
    held = {}
    returned = {}

    def activate(c, sums):
        tail = held[c][:, 2 * width :]
        weight = jnp.where(tail[:, 2:3] == me.astype(BF16), tail[:, 0:1], tail[:, 1:2])
        sums = [
            jnp.concatenate([s[:, a * part_units : (a + 1) * part_units] for s in sums], axis=1)
            for a in range(3)
        ]
        scaled_hidden, gate_pre, up_pre, route_part = activation_grads(sums, weight)
        kept[c] = [
            held[c][:, :width],
            held[c][:, width : 2 * width],
            scaled_hidden,
            gate_pre,
            up_pre,
            route_part,
        ]
        mark(up_pre)

    def to_input(c):
        gate_pre, up_pre = gate(*kept[c][3:5])
        slot_grad = (
            lax.dot_general(gate_pre, gate_mat, over_units, preferred_element_type=F32)
            + lax.dot_general(up_pre, up_mat, over_units, preferred_element_type=F32)
        ).astype(BF16)
        kept[c].append(mark(slot_grad))

    def give_back(c):
        route_part, slot_grad = gate(*kept[c][5:])
        back = jnp.concatenate(
            [slot_grad, jnp.broadcast_to(route_part, (route_part.shape[0], lanes))], axis=1
        )
        for i, r in enumerate(chunks[c]):
            one = back[i * capacity : (i + 1) * capacity]
            mark(one)
            if r:
                one = lax.ppermute(one, "expert", [(i, i ^ r) for i in range(groups)])
            returned[r] = one

    c_back = list(range(count))
    combined = [None]
    route_cols = {}

    def take_back(c):
        came = gate(*[returned[r] for r in chunks[c]])
        for r, one in zip(chunks[c], came):
            route_cols[r] = one[:, width]
        stacked = jnp.concatenate([one[:, :width] for one in came], axis=0)
        spread = jnp.concatenate([pick[r] for r in chunks[c]], axis=0)
        added = lax.dot_general(spread, stacked, over_rows, preferred_element_type=F32)
        if combined[0] is not None:
            added = combined[0] + added
        combined[0] = mark(added)

    if n_dp != 4:
        for c in range(count):
            held[c] = join([fetch(r) for r in chunks[c]])
            activate(c, [line_sum(forward(held[c], a), "dp", n_dp, place) for a in range(halves)])
            to_input(c)
            give_back(c)
    else:
        inward, across, outward = [(0, 1), (3, 2)], [(1, 2), (2, 1)], [(1, 0), (2, 3)]
        part, partly, total, spread_out = {}, {}, {}, {}
        arrived, crossed = {}, {}
        rows = {r: fetch(r) for r in reversed(chunks[0])}
        to_do = []

        def compute_part(k):
            c, half = divmod(k, halves)
            if half == 0:
                held[c] = join([rows[r] for r in chunks[c]])
                source = held[c]
            else:
                (source,) = gate(held[c])
            part[k] = mark(forward(source, half))

        def send(inner, outer):
            if inner is None:
                spread_out[outer] = lax.ppermute(total[outer], "dp", outward)
                return
            if outer is None:
                moved = lax.ppermute(part[inner], "dp", inward)
            else:
                both = mark(jnp.where(middle, total[outer], part[inner]))
                moved = lax.ppermute(both, "dp", inward + outward)
                spread_out[outer] = moved
            arrived[inner] = moved

        compute_part(0)
        send(0, None)
        for t in range(pieces + 4):
            if t == 0:
                compute_part(1)
                send(1, None)
            if 1 <= t <= pieces:
                k = t - 1
                (came,) = gate(arrived[k])
                partly[k] = mark((part[k].astype(F32) + came.astype(F32)).astype(BF16))
                crossed[k] = lax.ppermute(partly[k], "dp", across)
            c = {0: 1, 2: 2, 3: 3}.get(t)
            if c is not None and c < count:
                for r in chunks[c]:
                    rows[r] = fetch(r)
            if 1 <= t and t + 1 < pieces:
                compute_part(t + 1)
            if 2 <= t <= pieces + 1:
                k = t - 2
                (came,) = gate(crossed[k])
                total[k] = mark((partly[k].astype(F32) + came.astype(F32)).astype(BF16))
                if t + 1 >= pieces:
                    send(None, k)
            if 1 <= t and t + 1 < pieces:
                send(t + 1, t - 2 if t >= 2 else None)
            done = t - 4
            if done >= 0 and done % halves == halves - 1:
                c = done // halves
                to_do += [(activate, c), (to_input, c), (give_back, c)]
            if t >= pieces + 1 and c_back:
                take_back(c_back.pop(0))
            if to_do:
                step, c = to_do.pop(0)
                if step is activate:
                    own = [halves * c + a for a in range(halves)]
                    came = gate(*[spread_out[k] for k in own])
                    activate(c, [jnp.where(middle, total[k], a) for k, a in zip(own, came)])
                else:
                    step(c)
                if step is to_input and to_do and to_do[0][1] == c:
                    step, c = to_do.pop(0)
                    step(c)
        for step, c in to_do:
            step(c)
    for c in c_back[:-1]:
        take_back(c)
    kept = [kept[c] for c in range(count)]
    all_in, all_grad, all_hidden, all_gate, all_up = (
        jnp.concatenate([k[i] for k in kept], axis=0) for i in range(5)
    )
    grad_down = lax.dot_general(all_hidden, all_grad, over_rows, preferred_element_type=F32)
    grad_gate = lax.dot_general(all_in, all_gate, over_rows, preferred_element_type=F32)
    grad_up = lax.dot_general(all_in, all_up, over_rows, preferred_element_type=F32)
    grad_down, grad_gate, grad_up = (g.astype(BF16) for g in (grad_down, grad_gate, grad_up))
    mark((grad_down[:8, :128], grad_gate[:8, :128], grad_up[:8, :128]))
    take_back(c_back[-1])
    input_grad = combined[0].astype(BF16)
    route_cols = jnp.stack([route_cols[r] for r in range(groups)], axis=0)
    per_offset = jnp.einsum("rst,rs->tr", pick, route_cols, preferred_element_type=F32)
    route_grad = jnp.sum(jnp.where(named, per_offset[:, None, :], 0.0), axis=2).astype(BF16)
    return (
        input_grad,
        route_grad,
        grad_gate[None],
        grad_up[None],
        grad_down[None],
    )


def solution(mesh):
    placed = (
        P("expert", "dp"),
        P("expert", "dp"),
        P("expert", None),
        P("expert", None),
        P("expert", "dp", None),
        P("expert", "dp", None),
        P("expert", None, "dp"),
    )
    return jax.shard_map(
        body,
        mesh=mesh,
        in_specs=placed,
        out_specs=(
            P("expert", "dp"),
            P("expert", None),
            P("expert", "dp", None),
            P("expert", "dp", None),
            P("expert", None, "dp"),
        ),
        check_vma=False,
    )
```

```python
import jax
import jax.numpy as jnp
from jax import lax
from jax.sharding import PartitionSpec as P

BF16 = jnp.bfloat16
F32 = jnp.float32


def line_sum(part, axis, size, place):
    half = size // 2
    total = part
    for k in range(half - 1):
        pairs = [(k, k + 1), (size - 1 - k, size - 2 - k)]
        arrived = lax.ppermute(total, axis, pairs)
        total = (total.astype(F32) + arrived.astype(F32)).astype(BF16)
    arrived = lax.ppermute(total, axis, [(half - 1, half), (half, half - 1)])
    total = (total.astype(F32) + arrived.astype(F32)).astype(BF16)
    depth = jnp.where(place < half, half - 1 - place, place - half)
    for k in range(half - 1):
        pairs = [(half - 1 - k, half - 2 - k), (half + k, half + k + 1)]
        arrived = lax.ppermute(total, axis, pairs)
        total = jnp.where(depth == k + 1, arrived, total)
    return total


def activation_grads(sums, weight):
    pre_gate, pre_up, back_hidden = (one.astype(F32) for one in sums)
    sigmoid_gate = jax.nn.sigmoid(pre_gate)
    silu_gate = pre_gate * sigmoid_gate
    hidden = silu_gate * pre_up
    route_part = jnp.sum(hidden * back_hidden, axis=1, keepdims=True).astype(BF16)
    scale = weight.astype(F32)
    scaled_hidden = (scale * hidden).astype(BF16)
    gate_pre = (
        scale * back_hidden * pre_up * sigmoid_gate * (1.0 + pre_gate * (1.0 - sigmoid_gate))
    ).astype(BF16)
    up_pre = (scale * back_hidden * silu_gate).astype(BF16)
    return (scaled_hidden, gate_pre, up_pre, route_part)


def body(layer_input, out_grad, routes, gate_weights, w_gate, w_up, w_down):
    groups = lax.axis_size("expert")
    n_dp = lax.axis_size("dp")
    me = lax.axis_index("expert")
    place = lax.axis_index("dp")
    tokens, width = layer_input.shape
    choose = routes.shape[1]
    capacity = 2 * tokens * choose // groups
    per_chunk = max(1, groups // 4)
    offsets = [0, 1, 3, 5, 2, 4, 6, 7] if groups == 8 else list(range(groups))
    chunks = [offsets[i : i + per_chunk] for i in range(0, groups, per_chunk)]

    partner = me ^ jnp.arange(groups, dtype=jnp.int32)
    named = routes[:, :, None] == partner[None, None, :]
    chosen = jnp.any(named, axis=1)
    rank = jnp.cumsum(chosen.astype(jnp.int32), axis=0) - 1
    rank = jnp.where(chosen, rank, -1).T
    slot = jnp.arange(capacity, dtype=jnp.int32)
    pick = (rank[:, None, :] == slot[None, :, None]).astype(BF16)

    lanes = 128
    extra = jnp.concatenate([gate_weights, routes[:, :1].astype(BF16)], axis=1)
    extra = jnp.pad(extra, ((0, 0), (0, lanes - choose - 1)))
    packed = jnp.concatenate([layer_input, out_grad, extra], axis=1)

    gate_mat, up_mat, down_mat = w_gate[0], w_up[0], w_down[0]
    over_units = (((1,), (1,)), ((), ()))
    over_rows = (((0,), (0,)), ((), ()))

    middle = (place == n_dp // 2 - 1) | (place == n_dp // 2)

    last = [None]

    def gate(*values):
        if last[0] is None:
            return values
        return lax.optimization_barrier((*values, last[0]))[:-1]

    def mark(value):
        last[0] = value
        return value

    def fetch(r):
        (one,) = gate(pick[r])
        rows = jnp.dot(one, packed, preferred_element_type=F32).astype(BF16)
        mark(rows)
        if r:
            rows = lax.ppermute(rows, "expert", [(i, i ^ r) for i in range(groups)])
        return rows

    def join(rows):
        rows = gate(*rows)
        return rows[0] if len(rows) == 1 else jnp.concatenate(rows, axis=0)

    halves = 2
    part_units = w_gate.shape[2] // halves

    def forward(rows, half):
        cols = slice(half * part_units, (half + 1) * part_units)
        rows_in, rows_grad = rows[:, :width], rows[:, width : 2 * width]
        part_gate = jnp.dot(rows_in, gate_mat[:, cols], preferred_element_type=F32)
        part_up = jnp.dot(rows_in, up_mat[:, cols], preferred_element_type=F32)
        part_back = lax.dot_general(
            rows_grad, down_mat[cols], over_units, preferred_element_type=F32
        )
        return jnp.concatenate(
            [part_gate.astype(BF16), part_up.astype(BF16), part_back.astype(BF16)], axis=1
        )

    count = len(chunks)
    pieces = halves * count
    kept = {}
    held = {}
    returned = {}

    def activate(c, sums):
        tail = held[c][:, 2 * width :]
        weight = jnp.where(tail[:, 2:3] == me.astype(BF16), tail[:, 0:1], tail[:, 1:2])
        sums = [
            jnp.concatenate([s[:, a * part_units : (a + 1) * part_units] for s in sums], axis=1)
            for a in range(3)
        ]
        scaled_hidden, gate_pre, up_pre, route_part = activation_grads(sums, weight)
        kept[c] = [
            held[c][:, :width],
            held[c][:, width : 2 * width],
            scaled_hidden,
            gate_pre,
            up_pre,
            route_part,
        ]
        mark(up_pre)

    def to_input(c):
        gate_pre, up_pre = gate(*kept[c][3:5])
        slot_grad = (
            lax.dot_general(gate_pre, gate_mat, over_units, preferred_element_type=F32)
            + lax.dot_general(up_pre, up_mat, over_units, preferred_element_type=F32)
        ).astype(BF16)
        kept[c].append(mark(slot_grad))

    def give_back(c):
        route_part, slot_grad = gate(*kept[c][5:])
        back = jnp.concatenate(
            [slot_grad, jnp.broadcast_to(route_part, (route_part.shape[0], lanes))], axis=1
        )
        for i, r in enumerate(chunks[c]):
            one = back[i * capacity : (i + 1) * capacity]
            mark(one)
            if r:
                one = lax.ppermute(one, "expert", [(i, i ^ r) for i in range(groups)])
            returned[r] = one

    combined = [None]
    route_cols = {}

    gradients = {}
    counted = {}

    def add_gradient(which):
        first = counted.get(which, 0)
        counted[which] = count if len(kept) == count else 2
        left, right = ((2, 1), (0, 3), (0, 4))[which]
        these = [kept[c] for c in range(first, counted[which])]
        rows_left = jnp.concatenate([one[left] for one in these], axis=0)
        rows_right = jnp.concatenate([one[right] for one in these], axis=0)
        (rows_left,) = gate(rows_left)
        added = lax.dot_general(rows_left, rows_right, over_rows, preferred_element_type=F32)
        if first:
            added = added + gradients[which].astype(F32)
        gradients[which] = added.astype(BF16)
        if counted[which] < count:
            gradients[which] = mark(gradients[which])

    def take_back(chunk):
        came = gate(*[returned[r] for r in chunk])
        for r, one in zip(chunk, came):
            route_cols[r] = one[:, width]
        stacked = jnp.concatenate([one[:, :width] for one in came], axis=0)
        spread = jnp.concatenate([pick[r] for r in chunk], axis=0)
        added = lax.dot_general(spread, stacked, over_rows, preferred_element_type=F32)
        if combined[0] is not None:
            added = combined[0] + added
        combined[0] = mark(added)

    if n_dp != 4:
        for c in range(count):
            held[c] = join([fetch(r) for r in chunks[c]])
            activate(c, [line_sum(forward(held[c], a), "dp", n_dp, place) for a in range(halves)])
            to_input(c)
            give_back(c)
    else:
        inward, across, outward = [(0, 1), (3, 2)], [(1, 2), (2, 1)], [(1, 0), (2, 3)]
        part, partly, total, spread_out = {}, {}, {}, {}
        arrived, crossed = {}, {}
        early = chunks[0][1:] + (chunks[1] if count > 1 else []) + chunks[0][:1]
        rows = {r: fetch(r) for r in early}
        work = {
            5: [(activate, 0)],
            6: [(to_input, 0), (give_back, 0)],
            7: [(activate, 1), (to_input, 1)],
            8: [(give_back, 1), (take_back, chunks[0]), (add_gradient, 0)],
            9: [(activate, 2), (to_input, 2), (add_gradient, 1)],
            10: [(give_back, 2), (take_back, chunks[1]), (add_gradient, 2), (take_back, chunks[2])],
        }

        def compute_part(k):
            c, half = divmod(k, halves)
            if half == 0:
                held[c] = join([rows[r] for r in chunks[c]])
                source = held[c]
            else:
                (source,) = gate(held[c])
            part[k] = mark(forward(source, half))

        def send(inner, outer):
            if inner is None:
                spread_out[outer] = lax.ppermute(total[outer], "dp", outward)
                return
            if outer is None:
                moved = lax.ppermute(part[inner], "dp", inward)
            else:
                both = mark(jnp.where(middle, total[outer], part[inner]))
                moved = lax.ppermute(both, "dp", inward + outward)
                spread_out[outer] = moved
            arrived[inner] = moved

        def finish(c):
            own = [halves * c + a for a in range(halves)]
            came = gate(*[spread_out[k] for k in own])
            activate(c, [jnp.where(middle, total[k], a) for k, a in zip(own, came)])

        compute_part(0)
        send(0, None)
        for t in range(pieces + 3):
            if t == 0:
                compute_part(1)
                send(1, None)
            if 1 <= t <= pieces:
                k = t - 1
                (came,) = gate(arrived[k])
                partly[k] = mark((part[k].astype(F32) + came.astype(F32)).astype(BF16))
                crossed[k] = lax.ppermute(partly[k], "dp", across)
            c = {1: 2, 3: 3}.get(t)
            if c is not None and c < count:
                for r in chunks[c]:
                    rows[r] = fetch(r)
            if 1 <= t and t + 1 < pieces:
                compute_part(t + 1)
            if 2 <= t <= pieces + 1:
                k = t - 2
                (came,) = gate(crossed[k])
                total[k] = mark((partly[k].astype(F32) + came.astype(F32)).astype(BF16))
                if t + 1 >= pieces:
                    send(None, k)
            if 1 <= t and t + 1 < pieces:
                send(t + 1, t - 2 if t >= 2 else None)
            for step, c in work.get(t, ()):
                if step is activate:
                    finish(c)
                else:
                    step(c)
        finish(3)
        to_input(3)
        give_back(3)
    add_gradient(0)
    add_gradient(1)
    mark((gradients[0][:8, :128], gradients[1][:8, :128]))
    take_back(chunks[-1][:1])
    add_gradient(2)
    grad_down, grad_gate, grad_up = (gradients[which] for which in range(3))
    mark(grad_up[:8, :128])
    for r in offsets:
        if r not in route_cols:
            take_back([r])
    input_grad = combined[0].astype(BF16)
    route_cols = jnp.stack([route_cols[r] for r in range(groups)], axis=0)
    per_offset = jnp.einsum("rst,rs->tr", pick, route_cols, preferred_element_type=F32)
    route_grad = jnp.sum(jnp.where(named, per_offset[:, None, :], 0.0), axis=2).astype(BF16)
    return (
        input_grad,
        route_grad,
        grad_gate[None],
        grad_up[None],
        grad_down[None],
    )


def solution(mesh):
    placed = (
        P("expert", "dp"),
        P("expert", "dp"),
        P("expert", None),
        P("expert", None),
        P("expert", "dp", None),
        P("expert", "dp", None),
        P("expert", None, "dp"),
    )
    return jax.shard_map(
        body,
        mesh=mesh,
        in_specs=placed,
        out_specs=(
            P("expert", "dp"),
            P("expert", None),
            P("expert", "dp", None),
            P("expert", "dp", None),
            P("expert", None, "dp"),
        ),
        check_vma=False,
    )
```

```python
import functools

import jax
import jax.numpy as jnp
from jax import lax
from jax.experimental import pallas as pl
from jax.experimental.pallas import tpu as pltpu
from jax.sharding import PartitionSpec as P

BF16 = jnp.bfloat16
F32 = jnp.float32


def line_sum(part, axis, size, place):
    half = size // 2
    total = part
    for k in range(half - 1):
        pairs = [(k, k + 1), (size - 1 - k, size - 2 - k)]
        arrived = lax.ppermute(total, axis, pairs)
        total = (total.astype(F32) + arrived.astype(F32)).astype(BF16)
    arrived = lax.ppermute(total, axis, [(half - 1, half), (half, half - 1)])
    total = (total.astype(F32) + arrived.astype(F32)).astype(BF16)
    depth = jnp.where(place < half, half - 1 - place, place - half)
    for k in range(half - 1):
        pairs = [(half - 1 - k, half - 2 - k), (half + k, half + k + 1)]
        arrived = lax.ppermute(total, axis, pairs)
        total = jnp.where(depth == k + 1, arrived, total)
    return total


def activation_grads(sums, weight):
    pre_gate, pre_up, back_hidden = (one.astype(F32) for one in sums)
    sigmoid_gate = jax.nn.sigmoid(pre_gate)
    silu_gate = pre_gate * sigmoid_gate
    hidden = silu_gate * pre_up
    route_part = jnp.sum(hidden * back_hidden, axis=1, keepdims=True).astype(BF16)
    scale = weight.astype(F32)
    scaled_hidden = (scale * hidden).astype(BF16)
    gate_pre = (
        scale * back_hidden * pre_up * sigmoid_gate * (1.0 + pre_gate * (1.0 - sigmoid_gate))
    ).astype(BF16)
    up_pre = (scale * back_hidden * silu_gate).astype(BF16)
    return (scaled_hidden, gate_pre, up_pre, route_part)


LITTLE = pl.CostEstimate(flops=1, bytes_accessed=1, transcendentals=0)
LANES = 128
BLOCK = 256
OVER_LAST = (((1,), (1,)), ((), ()))


def params(mebibytes):
    return pltpu.CompilerParams(vmem_limit_bytes=mebibytes * 1024 * 1024)


def whole(shape):
    return pl.BlockSpec(shape, lambda *_: (0,) * len(shape))


def forward_kernel(n_rows, width, per_array, scalars, *refs):
    rows, (gate_ref, up_ref, down_ref, out_ref, *joined) = refs[:n_rows], refs[n_rows:]
    step = pl.program_id(0)
    rows_in = jnp.concatenate([ref[:, :width] for ref in rows], axis=0)
    rows_grad = jnp.concatenate([ref[:, width : 2 * width] for ref in rows], axis=0)
    results = (
        jnp.dot(rows_in, gate_ref[0], preferred_element_type=F32),
        jnp.dot(rows_in, up_ref[0], preferred_element_type=F32),
        lax.dot_general(rows_grad, down_ref[0], OVER_LAST, preferred_element_type=F32),
    )
    for a, result in enumerate(results):
        start = pl.multiple_of(a * per_array + step * BLOCK, BLOCK)
        out_ref[:, pl.ds(start, BLOCK)] = result.astype(BF16)
    for ref, value in zip(joined, (rows_in, rows_grad)):
        ref[...] = value


def forward_piece(scalars, rows, w_gate, w_up, w_down, half, per_array):
    width = w_gate.shape[1]
    steps = per_array // BLOCK
    total = sum(r.shape[0] for r in rows)
    outs = [(total, 3 * per_array)] + ([(total, width)] * 2 if half == 0 else [])
    across = pl.BlockSpec((1, width, BLOCK), lambda j: (0, 0, half * steps + j))
    down = pl.BlockSpec((1, BLOCK, width), lambda j: (0, half * steps + j, 0))
    return pl.pallas_call(
        functools.partial(forward_kernel, len(rows), width, per_array),
        grid=(steps,),
        in_specs=[pl.BlockSpec(memory_space=pltpu.SMEM)]
        + [whole(r.shape) for r in rows]
        + [across, across, down],
        out_specs=[whole(shape) for shape in outs],
        out_shape=[jax.ShapeDtypeStruct(shape, BF16) for shape in outs],
        compiler_params=params(28),
        cost_estimate=LITTLE,
    )(scalars, *rows, w_gate, w_up, w_down)


def add_kernel(a_ref, b_ref, out_ref):
    out_ref[...] = (a_ref[...].astype(F32) + b_ref[...].astype(F32)).astype(BF16)


def add_pieces(a, b):
    return pl.pallas_call(
        add_kernel,
        out_shape=jax.ShapeDtypeStruct(a.shape, BF16),
        compiler_params=params(8),
        cost_estimate=LITTLE,
    )(a, b)


def add_choose_kernel(middle_ref, a_ref, b_ref, other_ref, out_ref, both_ref):
    total = (a_ref[...].astype(F32) + b_ref[...].astype(F32)).astype(BF16)
    out_ref[...] = total
    both_ref[...] = jnp.where(middle_ref[0] == 1, total.astype(F32), other_ref[...].astype(F32)).astype(BF16)


def add_choose(middle, a, b, other):
    spec = pl.BlockSpec(memory_space=pltpu.VMEM)
    return pl.pallas_call(
        add_choose_kernel,
        in_specs=[pl.BlockSpec(memory_space=pltpu.SMEM), spec, spec, spec],
        out_specs=[spec, spec],
        out_shape=[jax.ShapeDtypeStruct(a.shape, BF16)] * 2,
        compiler_params=params(8),
        cost_estimate=LITTLE,
    )(middle, a, b, other)


def backward_kernel(n_rows, width, steps, scalars, *refs):
    own, refs = refs[:2], refs[2:]
    came, refs = refs[:2], refs[2:]
    extras, refs = refs[:n_rows], refs[n_rows:]
    gate_ref, up_ref, hidden_ref, gate_pre_ref, up_pre_ref = refs[:5]
    backs, (acc_ref, route_ref) = refs[5 : 5 + n_rows], refs[5 + n_rows :]
    step = pl.program_id(0)
    per_array = own[0].shape[1] // 3
    half = step // (steps // 2)
    start = (step % (steps // 2)) * BLOCK

    def load(a):
        cols = pl.ds(pl.multiple_of(a * per_array + start, BLOCK), BLOCK)
        first = jnp.where(scalars[0] == 1, own[0][:, cols].astype(F32), came[0][:, cols].astype(F32))
        second = jnp.where(scalars[0] == 1, own[1][:, cols].astype(F32), came[1][:, cols].astype(F32))
        return jnp.where(half == 0, first, second)

    tail = jnp.concatenate([ref[...] for ref in extras], axis=0).astype(F32)
    weight = jnp.where(tail[:, 2:3] == scalars[1].astype(F32), tail[:, 0:1], tail[:, 1:2])
    pre_gate, pre_up, back_hidden = load(0), load(1), load(2)
    sigmoid_gate = jax.nn.sigmoid(pre_gate)
    silu_gate = pre_gate * sigmoid_gate
    hidden = silu_gate * pre_up
    route = jnp.sum(hidden * back_hidden, axis=1, keepdims=True)
    hidden_ref[...] = (weight * hidden).astype(BF16)
    gate_pre = (
        weight * back_hidden * pre_up * sigmoid_gate * (1.0 + pre_gate * (1.0 - sigmoid_gate))
    ).astype(BF16)
    up_pre = (weight * back_hidden * silu_gate).astype(BF16)
    gate_pre_ref[...] = gate_pre
    up_pre_ref[...] = up_pre
    grad = lax.dot_general(
        gate_pre, gate_ref[0], OVER_LAST, preferred_element_type=F32
    ) + lax.dot_general(up_pre, up_ref[0], OVER_LAST, preferred_element_type=F32)

    @pl.when(step == 0)
    def _():
        acc_ref[...] = grad
        route_ref[...] = jnp.broadcast_to(route, route_ref.shape)

    @pl.when(step > 0)
    def _():
        acc_ref[...] += grad
        route_ref[...] += jnp.broadcast_to(route, route_ref.shape)

    @pl.when(step == steps - 1)
    def _():
        rows = backs[0].shape[0]
        for i, ref in enumerate(backs):
            ref[:, :width] = acc_ref[i * rows : (i + 1) * rows, :].astype(BF16)
            ref[:, width:] = route_ref[i * rows : (i + 1) * rows, :].astype(BF16)


def backward_chunk(scalars, own, came, rows, w_gate, w_up):
    width, units = w_gate.shape[1:]
    steps = units // BLOCK
    height = rows[0].shape[0]
    total = height * len(rows)
    across = pl.BlockSpec((1, width, BLOCK), lambda j: (0, 0, j))
    column = pl.BlockSpec((total, BLOCK), lambda j: (0, j))
    extra = pl.BlockSpec((height, LANES), lambda j: (0, 2 * width // LANES))
    back = (height, width + LANES)
    return pl.pallas_call(
        functools.partial(backward_kernel, len(rows), width, steps),
        grid=(steps,),
        in_specs=[pl.BlockSpec(memory_space=pltpu.SMEM)]
        + [whole(p.shape) for p in (*own, *came)]
        + [extra] * len(rows)
        + [across, across],
        out_specs=[column] * 3 + [whole(back)] * len(rows),
        out_shape=[jax.ShapeDtypeStruct((total, units), BF16)] * 3
        + [jax.ShapeDtypeStruct(back, BF16)] * len(rows),
        scratch_shapes=[pltpu.VMEM((total, width), F32), pltpu.VMEM((total, LANES), F32)],
        compiler_params=params(32),
        cost_estimate=LITTLE,
    )(scalars, *own, *came, *rows, w_gate, w_up)


def body(layer_input, out_grad, routes, gate_weights, w_gate, w_up, w_down):
    groups = lax.axis_size("expert")
    n_dp = lax.axis_size("dp")
    me = lax.axis_index("expert")
    place = lax.axis_index("dp")
    tokens, width = layer_input.shape
    choose = routes.shape[1]
    capacity = 2 * tokens * choose // groups
    per_chunk = max(1, groups // 4)
    offsets = [0, 1, 3, 5, 2, 4, 6, 7] if groups == 8 else list(range(groups))
    chunks = [offsets[i : i + per_chunk] for i in range(0, groups, per_chunk)]

    partner = me ^ jnp.arange(groups, dtype=jnp.int32)
    named = routes[:, :, None] == partner[None, None, :]
    chosen = jnp.any(named, axis=1)
    rank = jnp.cumsum(chosen.astype(jnp.int32), axis=0) - 1
    rank = jnp.where(chosen, rank, -1).T
    slot = jnp.arange(capacity, dtype=jnp.int32)
    pick = (rank[:, None, :] == slot[None, :, None]).astype(BF16)

    lanes = 128
    extra = jnp.concatenate([gate_weights, routes[:, :1].astype(BF16)], axis=1)
    extra = jnp.pad(extra, ((0, 0), (0, lanes - choose - 1)))
    packed = jnp.concatenate([layer_input, out_grad, extra], axis=1)

    gate_mat, up_mat, down_mat = w_gate[0], w_up[0], w_down[0]
    over_units = (((1,), (1,)), ((), ()))
    over_rows = (((0,), (0,)), ((), ()))

    middle = (place == n_dp // 2 - 1) | (place == n_dp // 2)

    last = [None]

    def gate(*values):
        if last[0] is None:
            return values
        return lax.optimization_barrier((*values, last[0]))[:-1]

    def mark(value):
        last[0] = value
        return value

    def fetch(r):
        (one,) = gate(pick[r])
        rows = jnp.dot(one, packed, preferred_element_type=F32).astype(BF16)
        mark(rows)
        if r:
            rows = lax.ppermute(rows, "expert", [(i, i ^ r) for i in range(groups)])
        return rows

    def join(rows):
        rows = gate(*rows)
        return rows[0] if len(rows) == 1 else jnp.concatenate(rows, axis=0)

    halves = 2
    part_units = w_gate.shape[2] // halves

    def forward(rows, half):
        cols = slice(half * part_units, (half + 1) * part_units)
        rows_in, rows_grad = rows[:, :width], rows[:, width : 2 * width]
        part_gate = jnp.dot(rows_in, gate_mat[:, cols], preferred_element_type=F32)
        part_up = jnp.dot(rows_in, up_mat[:, cols], preferred_element_type=F32)
        part_back = lax.dot_general(
            rows_grad, down_mat[cols], over_units, preferred_element_type=F32
        )
        return jnp.concatenate(
            [part_gate.astype(BF16), part_up.astype(BF16), part_back.astype(BF16)], axis=1
        )

    count = len(chunks)
    pieces = halves * count
    kept = {}
    held = {}
    returned = {}

    def activate(c, sums):
        tail = held[c][:, 2 * width :]
        weight = jnp.where(tail[:, 2:3] == me.astype(BF16), tail[:, 0:1], tail[:, 1:2])
        sums = [
            jnp.concatenate([s[:, a * part_units : (a + 1) * part_units] for s in sums], axis=1)
            for a in range(3)
        ]
        scaled_hidden, gate_pre, up_pre, route_part = activation_grads(sums, weight)
        kept[c] = [
            held[c][:, :width],
            held[c][:, width : 2 * width],
            scaled_hidden,
            gate_pre,
            up_pre,
            route_part,
        ]
        mark(up_pre)

    def to_input(c):
        gate_pre, up_pre = gate(*kept[c][3:5])
        slot_grad = (
            lax.dot_general(gate_pre, gate_mat, over_units, preferred_element_type=F32)
            + lax.dot_general(up_pre, up_mat, over_units, preferred_element_type=F32)
        ).astype(BF16)
        kept[c].append(mark(slot_grad))

    def give_back(c):
        route_part, slot_grad = gate(*kept[c][5:])
        back = jnp.concatenate(
            [slot_grad, jnp.broadcast_to(route_part, (route_part.shape[0], lanes))], axis=1
        )
        for i, r in enumerate(chunks[c]):
            one = back[i * capacity : (i + 1) * capacity]
            mark(one)
            if r:
                one = lax.ppermute(one, "expert", [(i, i ^ r) for i in range(groups)])
            returned[r] = one

    combined = [None]
    route_cols = {}

    gradients = {}
    counted = {}

    def add_gradient(which):
        first = counted.get(which, 0)
        counted[which] = count if len(kept) == count else 2
        left, right = ((2, 1), (0, 3), (0, 4))[which]
        these = [kept[c] for c in range(first, counted[which])]
        rows_left = jnp.concatenate([one[left] for one in these], axis=0)
        rows_right = jnp.concatenate([one[right] for one in these], axis=0)
        (rows_left,) = gate(rows_left)
        added = lax.dot_general(rows_left, rows_right, over_rows, preferred_element_type=F32)
        if first:
            added = added + gradients[which].astype(F32)
        gradients[which] = added.astype(BF16)
        if counted[which] < count:
            gradients[which] = mark(gradients[which])

    def take_back(chunk):
        came = gate(*[returned[r] for r in chunk])
        for r, one in zip(chunk, came):
            route_cols[r] = one[:, width]
        stacked = jnp.concatenate([one[:, :width] for one in came], axis=0)
        spread = jnp.concatenate([pick[r] for r in chunk], axis=0)
        added = lax.dot_general(spread, stacked, over_rows, preferred_element_type=F32)
        if combined[0] is not None:
            added = combined[0] + added
        combined[0] = mark(added)

    if n_dp != 4:
        for c in range(count):
            held[c] = join([fetch(r) for r in chunks[c]])
            activate(c, [line_sum(forward(held[c], a), "dp", n_dp, place) for a in range(halves)])
            to_input(c)
            give_back(c)
    else:
        inward, across, outward = [(0, 1), (3, 2)], [(1, 2), (2, 1)], [(1, 0), (2, 3)]
        part, partly, total, spread_out = {}, {}, {}, {}
        arrived, crossed, joined = {}, {}, {}
        scalars = jnp.stack([middle.astype(jnp.int32), me.astype(jnp.int32)])
        early = chunks[0][1:] + chunks[1] + chunks[0][:1]
        rows = {r: fetch(r) for r in early}

        def compute_part(k):
            c, half = divmod(k, halves)
            if half == 0:
                held[c] = gate(*[rows[r] for r in chunks[c]])
            (ready,) = gate(scalars)
            part[k], *wide = forward_piece(
                ready, held[c], w_gate, w_up, w_down, half, part_units
            )
            mark(part[k])
            if half == 0:
                joined[c] = wide

        def finish(c):
            own = [halves * c + a for a in range(halves)]
            came = gate(*[spread_out[k] for k in own])
            results = backward_chunk(
                scalars, [total[k] for k in own], came, held[c], w_gate, w_up
            )
            kept[c] = [*joined[c], *results[:3]]
            mark(results[0])
            for r, one in zip(chunks[c], results[3:]):
                if r:
                    one = lax.ppermute(one, "expert", [(i, i ^ r) for i in range(groups)])
                returned[r] = one

        work = {
            5: [(finish, 0)],
            7: [(finish, 1), (take_back, chunks[0])],
            8: [(add_gradient, 0)],
            9: [(finish, 2), (take_back, chunks[1]), (add_gradient, 1), (add_gradient, 2)],
        }
        compute_part(0)
        arrived[0] = lax.ppermute(part[0], "dp", inward)
        compute_part(1)
        arrived[1] = lax.ppermute(part[1], "dp", inward)
        for r in chunks[2]:
            rows[r] = fetch(r)
        for t in range(1, pieces + 2):
            if t <= pieces:
                (came,) = gate(arrived[t - 1])
                partly[t - 1] = mark(add_pieces(part[t - 1], came))
                crossed[t - 1] = lax.ppermute(partly[t - 1], "dp", across)
            if t + 1 < pieces:
                compute_part(t + 1)
            if t == 1:
                arrived[2] = lax.ppermute(part[2], "dp", inward)
                for r in chunks[3]:
                    rows[r] = fetch(r)
            else:
                k = t - 2
                (came,) = gate(crossed[k])
                if t + 1 < pieces:
                    total[k], both = add_choose(scalars, partly[k], came, part[t + 1])
                    mark(both)
                    arrived[t + 1] = lax.ppermute(both, "dp", inward + outward)
                    spread_out[k] = arrived[t + 1]
                else:
                    total[k] = mark(add_pieces(partly[k], came))
                    spread_out[k] = lax.ppermute(total[k], "dp", outward)
            for step, c in work.get(t, ()):
                step(c)
        finish(3)
        take_back(chunks[2])
    add_gradient(0)
    add_gradient(1)
    mark((gradients[0][:8, :128], gradients[1][:8, :128]))
    take_back(chunks[-1][:1])
    add_gradient(2)
    grad_down, grad_gate, grad_up = (gradients[which] for which in range(3))
    mark(grad_up[:8, :128])
    for r in offsets:
        if r not in route_cols:
            take_back([r])
    input_grad = combined[0].astype(BF16)
    route_cols = jnp.stack([route_cols[r] for r in range(groups)], axis=0)
    per_offset = jnp.einsum("rst,rs->tr", pick, route_cols, preferred_element_type=F32)
    route_grad = jnp.sum(jnp.where(named, per_offset[:, None, :], 0.0), axis=2).astype(BF16)
    return (
        input_grad,
        route_grad,
        grad_gate[None],
        grad_up[None],
        grad_down[None],
    )


def solution(mesh):
    placed = (
        P("expert", "dp"),
        P("expert", "dp"),
        P("expert", None),
        P("expert", None),
        P("expert", "dp", None),
        P("expert", "dp", None),
        P("expert", None, "dp"),
    )
    return jax.shard_map(
        body,
        mesh=mesh,
        in_specs=placed,
        out_specs=(
            P("expert", "dp"),
            P("expert", None),
            P("expert", "dp", None),
            P("expert", "dp", None),
            P("expert", None, "dp"),
        ),
        check_vma=False,
    )
```

```python
import functools

import jax
import jax.numpy as jnp
from jax import lax
from jax.experimental import pallas as pl
from jax.experimental.pallas import tpu as pltpu
from jax.sharding import PartitionSpec as P

BF16 = jnp.bfloat16
F32 = jnp.float32


def line_sum(part, axis, size, place):
    half = size // 2
    total = part
    for k in range(half - 1):
        pairs = [(k, k + 1), (size - 1 - k, size - 2 - k)]
        arrived = lax.ppermute(total, axis, pairs)
        total = (total.astype(F32) + arrived.astype(F32)).astype(BF16)
    arrived = lax.ppermute(total, axis, [(half - 1, half), (half, half - 1)])
    total = (total.astype(F32) + arrived.astype(F32)).astype(BF16)
    depth = jnp.where(place < half, half - 1 - place, place - half)
    for k in range(half - 1):
        pairs = [(half - 1 - k, half - 2 - k), (half + k, half + k + 1)]
        arrived = lax.ppermute(total, axis, pairs)
        total = jnp.where(depth == k + 1, arrived, total)
    return total


def activation_grads(sums, weight):
    pre_gate, pre_up, back_hidden = (one.astype(F32) for one in sums)
    sigmoid_gate = jax.nn.sigmoid(pre_gate)
    silu_gate = pre_gate * sigmoid_gate
    hidden = silu_gate * pre_up
    route_part = jnp.sum(hidden * back_hidden, axis=1, keepdims=True).astype(BF16)
    scale = weight.astype(F32)
    scaled_hidden = (scale * hidden).astype(BF16)
    gate_pre = (
        scale * back_hidden * pre_up * sigmoid_gate * (1.0 + pre_gate * (1.0 - sigmoid_gate))
    ).astype(BF16)
    up_pre = (scale * back_hidden * silu_gate).astype(BF16)
    return (scaled_hidden, gate_pre, up_pre, route_part)


LITTLE = pl.CostEstimate(flops=1, bytes_accessed=1, transcendentals=0)
LANES = 128
BLOCK = 256
OVER_LAST = (((1,), (1,)), ((), ()))


def params(mebibytes):
    return pltpu.CompilerParams(vmem_limit_bytes=mebibytes * 1024 * 1024)


def whole(shape):
    return pl.BlockSpec(shape, lambda *_: (0,) * len(shape))


def forward_kernel(n_rows, width, per_array, scalars, *refs):
    rows, (gate_ref, up_ref, down_ref, out_ref, *joined) = refs[:n_rows], refs[n_rows:]
    step = pl.program_id(0)
    rows_in = jnp.concatenate([ref[:, :width] for ref in rows], axis=0)
    rows_grad = jnp.concatenate([ref[:, width : 2 * width] for ref in rows], axis=0)
    results = (
        jnp.dot(rows_in, gate_ref[0], preferred_element_type=F32),
        jnp.dot(rows_in, up_ref[0], preferred_element_type=F32),
        lax.dot_general(rows_grad, down_ref[0], OVER_LAST, preferred_element_type=F32),
    )
    for a, result in enumerate(results):
        start = pl.multiple_of(a * per_array + step * BLOCK, BLOCK)
        out_ref[:, pl.ds(start, BLOCK)] = result.astype(BF16)
    for ref, value in zip(joined, (rows_in, rows_grad)):
        ref[...] = value


def forward_piece(scalars, rows, height, w_gate, w_up, w_down, half, per_array):
    width = w_gate.shape[1]
    steps = per_array // BLOCK
    total = height * len(rows)
    outs = [(total, 3 * per_array)] + ([(total, width)] * 2 if half == 0 else [])
    across = pl.BlockSpec((1, width, BLOCK), lambda j: (0, 0, half * steps + j))
    down = pl.BlockSpec((1, BLOCK, width), lambda j: (0, half * steps + j, 0))
    return pl.pallas_call(
        functools.partial(forward_kernel, len(rows), width, per_array),
        grid=(steps,),
        in_specs=[pl.BlockSpec(memory_space=pltpu.SMEM)]
        + [whole((height, r.shape[1])) for r in rows]
        + [across, across, down],
        out_specs=[whole(shape) for shape in outs],
        out_shape=[jax.ShapeDtypeStruct(shape, BF16) for shape in outs],
        compiler_params=params(28),
        cost_estimate=LITTLE,
    )(scalars, *rows, w_gate, w_up, w_down)


def add_kernel(a_ref, b_ref, out_ref):
    out_ref[...] = (a_ref[...].astype(F32) + b_ref[...].astype(F32)).astype(BF16)


def add_pieces(a, b):
    return pl.pallas_call(
        add_kernel,
        out_shape=jax.ShapeDtypeStruct(a.shape, BF16),
        compiler_params=params(8),
        cost_estimate=LITTLE,
    )(a, b)


def add_choose_kernel(middle_ref, a_ref, b_ref, other_ref, out_ref, both_ref):
    total = (a_ref[...].astype(F32) + b_ref[...].astype(F32)).astype(BF16)
    out_ref[...] = total
    both_ref[...] = jnp.where(middle_ref[0] == 1, total.astype(F32), other_ref[...].astype(F32)).astype(BF16)


def add_choose(middle, a, b, other):
    spec = pl.BlockSpec(memory_space=pltpu.VMEM)
    return pl.pallas_call(
        add_choose_kernel,
        in_specs=[pl.BlockSpec(memory_space=pltpu.SMEM), spec, spec, spec],
        out_specs=[spec, spec],
        out_shape=[jax.ShapeDtypeStruct(a.shape, BF16)] * 2,
        compiler_params=params(8),
        cost_estimate=LITTLE,
    )(middle, a, b, other)


def backward_kernel(n_rows, width, first, scalars, own_ref, came_ref, *refs):
    extras, refs = refs[:n_rows], refs[n_rows:]
    (gate_ref, up_ref), refs = refs[:2], refs[2:]
    if not first:
        (grad_in, route_in), refs = refs[:2], refs[5:]
    hidden_ref, gate_pre_ref, up_pre_ref = refs[:3]
    per_array = own_ref.shape[1] // 3

    def load(a):
        cols = slice(a * per_array, (a + 1) * per_array)
        return jnp.where(
            scalars[0] == 1, own_ref[:, cols].astype(F32), came_ref[:, cols].astype(F32)
        )

    tail = jnp.concatenate([ref[...] for ref in extras], axis=0).astype(F32)
    weight = jnp.where(tail[:, 2:3] == scalars[1].astype(F32), tail[:, 0:1], tail[:, 1:2])
    pre_gate, pre_up, back_hidden = load(0), load(1), load(2)
    sigmoid_gate = jax.nn.sigmoid(pre_gate)
    silu_gate = pre_gate * sigmoid_gate
    hidden = silu_gate * pre_up
    route = jnp.sum(hidden * back_hidden, axis=1, keepdims=True)
    hidden_ref[...] = (weight * hidden).astype(BF16)
    gate_pre = (
        weight * back_hidden * pre_up * sigmoid_gate * (1.0 + pre_gate * (1.0 - sigmoid_gate))
    ).astype(BF16)
    up_pre = (weight * back_hidden * silu_gate).astype(BF16)
    gate_pre_ref[...] = gate_pre
    up_pre_ref[...] = up_pre
    grad = lax.dot_general(
        gate_pre, gate_ref[0], OVER_LAST, preferred_element_type=F32
    ) + lax.dot_general(up_pre, up_ref[0], OVER_LAST, preferred_element_type=F32)
    if first:
        grad_ref, route_ref = refs[3:]
        grad_ref[...] = grad
        route_ref[...] = jnp.broadcast_to(route, route_ref.shape)
        return
    backs = refs[3:]
    grad = grad + grad_in[...]
    routes = route_in[...] + jnp.broadcast_to(route, route_in.shape)
    rows = backs[0].shape[0]
    for i, ref in enumerate(backs):
        ref[:, :width] = grad[i * rows : (i + 1) * rows, :].astype(BF16)
        ref[:, width:] = routes[i * rows : (i + 1) * rows, :].astype(BF16)


def backward_piece(scalars, own, came, rows, height, w_gate, w_up, half, before):
    width, units = w_gate.shape[1:]
    total = height * len(rows)
    per_array = own.shape[1] // 3
    across = pl.BlockSpec((1, width, per_array), lambda j: (0, 0, half))
    column = pl.BlockSpec((total, per_array), lambda j: (0, half))
    extra = pl.BlockSpec((height, LANES), lambda j: (0, 2 * width // LANES))
    sums = [(total, width), (total, LANES)]
    back = (height, width + LANES)
    in_specs = [pl.BlockSpec(memory_space=pltpu.SMEM), whole(own.shape), whole(came.shape)]
    in_specs += [extra] * len(rows) + [across, across]
    operands = [scalars, own, came, *rows, w_gate, w_up]
    aliases = {}
    if half:
        in_specs += [whole(shape) for shape in sums]
        in_specs += [pl.BlockSpec(memory_space=pl.ANY)] * 3
        operands += [*before[3:], *before[:3]]
        aliases = {len(operands) - 3 + i: i for i in range(3)}
        outs = [whole(back)] * len(rows)
        shapes = [jax.ShapeDtypeStruct(back, BF16)] * len(rows)
    else:
        outs = [whole(shape) for shape in sums]
        shapes = [jax.ShapeDtypeStruct(shape, F32) for shape in sums]
    return pl.pallas_call(
        functools.partial(backward_kernel, len(rows), width, half == 0),
        grid=(1,),
        in_specs=in_specs,
        out_specs=[column] * 3 + outs,
        out_shape=[jax.ShapeDtypeStruct((total, units), BF16)] * 3 + shapes,
        input_output_aliases=aliases,
        compiler_params=params(32),
        cost_estimate=LITTLE,
    )(*operands)


def tie_kernel(*refs):
    refs[-1][...] = jnp.zeros(refs[-1].shape, jnp.int32)


def tie(*arrays):
    return pl.pallas_call(
        tie_kernel,
        in_specs=[pl.BlockSpec(memory_space=pl.ANY)] * len(arrays),
        out_shape=jax.ShapeDtypeStruct((8, LANES), jnp.int32),
        cost_estimate=LITTLE,
    )(*arrays)


def body(layer_input, out_grad, routes, gate_weights, w_gate, w_up, w_down):
    groups = lax.axis_size("expert")
    n_dp = lax.axis_size("dp")
    me = lax.axis_index("expert")
    place = lax.axis_index("dp")
    tokens, width = layer_input.shape
    choose = routes.shape[1]
    capacity = 2 * tokens * choose // groups
    per_chunk = max(1, groups // 4)
    offsets = list(range(groups))
    chunks = [offsets[i : i + per_chunk] for i in range(0, groups, per_chunk)]

    partner = me ^ jnp.arange(groups, dtype=jnp.int32)
    named = routes[:, :, None] == partner[None, None, :]
    chosen = jnp.any(named, axis=1)
    rank = jnp.cumsum(chosen.astype(jnp.int32), axis=0) - 1
    rank = jnp.where(chosen, rank, -1).T
    slot = jnp.arange(capacity, dtype=jnp.int32)
    pick = (rank[:, None, :] == slot[None, :, None]).astype(BF16)

    lanes = 128
    extra = jnp.concatenate([gate_weights, routes[:, :1].astype(BF16)], axis=1)
    extra = jnp.pad(extra, ((0, 0), (0, lanes - choose - 1)))
    packed = jnp.concatenate([layer_input, out_grad, extra], axis=1)

    gate_mat, up_mat, down_mat = w_gate[0], w_up[0], w_down[0]
    over_units = (((1,), (1,)), ((), ()))
    over_rows = (((0,), (0,)), ((), ()))

    middle = (place == n_dp // 2 - 1) | (place == n_dp // 2)

    last = [None]

    def gate(*values):
        if last[0] is None:
            return values
        return lax.optimization_barrier((*values, last[0]))[:-1]

    def mark(value):
        last[0] = value
        return value

    def fetch(r):
        (one,) = gate(pick[r])
        rows = jnp.dot(one, packed, preferred_element_type=F32).astype(BF16)
        mark(rows)
        if r:
            rows = lax.ppermute(rows, "expert", [(i, i ^ r) for i in range(groups)])
        return rows

    def join(rows):
        rows = gate(*rows)
        return rows[0] if len(rows) == 1 else jnp.concatenate(rows, axis=0)

    halves = 2
    part_units = w_gate.shape[2] // halves

    def forward(rows, half):
        cols = slice(half * part_units, (half + 1) * part_units)
        rows_in, rows_grad = rows[:, :width], rows[:, width : 2 * width]
        part_gate = jnp.dot(rows_in, gate_mat[:, cols], preferred_element_type=F32)
        part_up = jnp.dot(rows_in, up_mat[:, cols], preferred_element_type=F32)
        part_back = lax.dot_general(
            rows_grad, down_mat[cols], over_units, preferred_element_type=F32
        )
        return jnp.concatenate(
            [part_gate.astype(BF16), part_up.astype(BF16), part_back.astype(BF16)], axis=1
        )

    count = len(chunks)
    pieces = halves * count
    kept = {}
    held = {}
    returned = {}

    def activate(c, sums):
        tail = held[c][:, 2 * width :]
        weight = jnp.where(tail[:, 2:3] == me.astype(BF16), tail[:, 0:1], tail[:, 1:2])
        sums = [
            jnp.concatenate([s[:, a * part_units : (a + 1) * part_units] for s in sums], axis=1)
            for a in range(3)
        ]
        scaled_hidden, gate_pre, up_pre, route_part = activation_grads(sums, weight)
        kept[c] = [
            held[c][:, :width],
            held[c][:, width : 2 * width],
            scaled_hidden,
            gate_pre,
            up_pre,
            route_part,
        ]
        mark(up_pre)

    def to_input(c):
        gate_pre, up_pre = gate(*kept[c][3:5])
        slot_grad = (
            lax.dot_general(gate_pre, gate_mat, over_units, preferred_element_type=F32)
            + lax.dot_general(up_pre, up_mat, over_units, preferred_element_type=F32)
        ).astype(BF16)
        kept[c].append(mark(slot_grad))

    def give_back(c):
        route_part, slot_grad = gate(*kept[c][5:])
        back = jnp.concatenate(
            [slot_grad, jnp.broadcast_to(route_part, (route_part.shape[0], lanes))], axis=1
        )
        for i, r in enumerate(chunks[c]):
            one = back[i * capacity : (i + 1) * capacity]
            mark(one)
            if r:
                one = lax.ppermute(one, "expert", [(i, i ^ r) for i in range(groups)])
            returned[r] = one

    combined = [None]
    route_cols = {}

    gradients = {}
    counted = {}

    def add_gradient(which):
        first = counted.get(which, 0)
        counted[which] = len(kept)
        left, right = ((2, 1), (0, 3), (0, 4))[which]
        these = [kept[c] for c in range(first, counted[which])]
        rows_left = jnp.concatenate([one[left] for one in these], axis=0)
        rows_right = jnp.concatenate([one[right] for one in these], axis=0)
        (rows_left,) = gate(rows_left)
        added = lax.dot_general(rows_left, rows_right, over_rows, preferred_element_type=F32)
        if first:
            added = added + gradients[which].astype(F32)
        gradients[which] = added.astype(BF16)
        if counted[which] < count:
            gradients[which] = mark(gradients[which])

    def take_back(chunk):
        came = gate(*[returned[r] for r in chunk])
        for r, one in zip(chunk, came):
            route_cols[r] = one[:, width]
        stacked = jnp.concatenate([one[:, :width] for one in came], axis=0)
        spread = jnp.concatenate([pick[r] for r in chunk], axis=0)
        added = lax.dot_general(spread, stacked, over_rows, preferred_element_type=F32)
        if combined[0] is not None:
            added = combined[0] + added
        combined[0] = mark(added)

    if n_dp != 4:
        for c in range(count):
            held[c] = join([fetch(r) for r in chunks[c]])
            activate(c, [line_sum(forward(held[c], a), "dp", n_dp, place) for a in range(halves)])
            to_input(c)
            give_back(c)
    else:
        inward, across, outward = [(0, 1), (3, 2)], [(1, 2), (2, 1)], [(1, 0), (2, 3)]
        part, partly, total, spread_out = {}, {}, {}, {}
        arrived, crossed, joined = {}, {}, {}
        scalars = jnp.stack([middle.astype(jnp.int32), me.astype(jnp.int32)])
        pairs = {}

        def fetch_pair(c):
            r = chunks[c][0]
            (both,) = gate(pick[r : r + 2].reshape(2 * capacity, tokens))
            sent = mark(jnp.dot(both, packed, preferred_element_type=F32).astype(BF16))
            pairs[c] = lax.ppermute(sent, "expert", [(i, i ^ r) for i in range(groups)])

        def hand_on(c):
            (pairs[c],) = gate(pairs[c])
            other = mark(pairs[c][capacity:])
            rows[c] = [
                pairs[c],
                lax.ppermute(other, "expert", [(i, i ^ 1) for i in range(groups)]),
            ]

        rows = {}
        fetch_pair(1)
        fetch_pair(2)
        from_core = fetch(1)
        rows[0] = [fetch(0), from_core]

        def compute_part(k):
            c, half = divmod(k, halves)
            if half == 0:
                held[c] = gate(*rows[c])
            (ready,) = gate(scalars)
            part[k], *wide = forward_piece(
                ready, held[c], capacity, w_gate, w_up, w_down, half, part_units
            )
            mark(part[k])
            if half == 0:
                joined[c] = wide

        begun = {}

        def finish(k):
            c, half = divmod(k, halves)
            (came,) = gate(spread_out[k])
            results = backward_piece(
                scalars, total[k], came, held[c], capacity, w_gate, w_up, half, begun.get(c)
            )
            mark(results[3])
            if half == 0:
                begun[c] = results
                return
            kept[c] = [*joined[c], *results[:3]]
            for r, one in zip(chunks[c], results[3:]):
                if r:
                    one = lax.ppermute(one, "expert", [(i, i ^ r) for i in range(groups)])
                returned[r] = one

        work = {
            1: [(fetch_pair, 3)],
            4: [(finish, 0)],
            5: [(finish, 1)],
            6: [(finish, 2)],
            7: [(finish, 3), (take_back, chunks[0])],
            8: [(finish, 4)],
            9: [(finish, 5), (add_gradient, 0), (take_back, chunks[1])],
        }
        compute_part(0)
        arrived[0] = lax.ppermute(part[0], "dp", inward)
        compute_part(1)
        arrived[1] = lax.ppermute(part[1], "dp", inward)
        for t in range(1, pieces + 2):
            if t <= pieces:
                (came,) = gate(arrived[t - 1])
                partly[t - 1] = mark(add_pieces(part[t - 1], came))
                crossed[t - 1] = lax.ppermute(partly[t - 1], "dp", across)
            if t in (1, 2, 4):
                hand_on(1 if t == 1 else t // 2 + 1)
            if t + 1 < pieces:
                compute_part(t + 1)
            if t == 1:
                arrived[2] = lax.ppermute(part[2], "dp", inward)
            else:
                k = t - 2
                (came,) = gate(crossed[k])
                if t + 1 < pieces:
                    total[k], both = add_choose(scalars, partly[k], came, part[t + 1])
                    mark(both)
                    arrived[t + 1] = lax.ppermute(both, "dp", inward + outward)
                    spread_out[k] = arrived[t + 1]
                else:
                    total[k] = mark(add_pieces(partly[k], came))
                    spread_out[k] = lax.ppermute(total[k], "dp", outward)
            for step, c in work.get(t, ()):
                step(c)
        finish(6)
        add_gradient(1)
        add_gradient(2)
        finish(7)
        take_back(chunks[2])
    for which in range(3):
        add_gradient(which)
    grad_down, grad_gate, grad_up = (gradients[which] for which in range(3))
    mark(tie(grad_down, grad_gate, grad_up))
    if len(chunks[-1]) == 2:
        take_back(chunks[-1])
    else:
        take_back([r for r in offsets if r not in route_cols])
    input_grad = combined[0].astype(BF16)
    route_cols = jnp.stack([route_cols[r] for r in range(groups)], axis=0)
    per_offset = jnp.einsum("rst,rs->tr", pick, route_cols, preferred_element_type=F32)
    route_grad = jnp.sum(jnp.where(named, per_offset[:, None, :], 0.0), axis=2).astype(BF16)
    return (
        input_grad,
        route_grad,
        grad_gate[None],
        grad_up[None],
        grad_down[None],
    )


def solution(mesh):
    placed = (
        P("expert", "dp"),
        P("expert", "dp"),
        P("expert", None),
        P("expert", None),
        P("expert", "dp", None),
        P("expert", "dp", None),
        P("expert", None, "dp"),
    )
    return jax.shard_map(
        body,
        mesh=mesh,
        in_specs=placed,
        out_specs=(
            P("expert", "dp"),
            P("expert", None),
            P("expert", "dp", None),
            P("expert", "dp", None),
            P("expert", None, "dp"),
        ),
        check_vma=False,
    )
```

```python
import functools

import jax
import jax.numpy as jnp
from jax import lax
from jax.experimental import pallas as pl
from jax.experimental.pallas import tpu as pltpu
from jax.sharding import PartitionSpec as P

BF16 = jnp.bfloat16
F32 = jnp.float32


def line_sum(part, axis, size, place):
    half = size // 2
    total = part
    for k in range(half - 1):
        pairs = [(k, k + 1), (size - 1 - k, size - 2 - k)]
        arrived = lax.ppermute(total, axis, pairs)
        total = (total.astype(F32) + arrived.astype(F32)).astype(BF16)
    arrived = lax.ppermute(total, axis, [(half - 1, half), (half, half - 1)])
    total = (total.astype(F32) + arrived.astype(F32)).astype(BF16)
    depth = jnp.where(place < half, half - 1 - place, place - half)
    for k in range(half - 1):
        pairs = [(half - 1 - k, half - 2 - k), (half + k, half + k + 1)]
        arrived = lax.ppermute(total, axis, pairs)
        total = jnp.where(depth == k + 1, arrived, total)
    return total


def activation_grads(sums, weight):
    pre_gate, pre_up, back_hidden = (one.astype(F32) for one in sums)
    sigmoid_gate = jax.nn.sigmoid(pre_gate)
    silu_gate = pre_gate * sigmoid_gate
    hidden = silu_gate * pre_up
    route_part = jnp.sum(hidden * back_hidden, axis=1, keepdims=True).astype(BF16)
    scale = weight.astype(F32)
    scaled_hidden = (scale * hidden).astype(BF16)
    gate_pre = (
        scale * back_hidden * pre_up * sigmoid_gate * (1.0 + pre_gate * (1.0 - sigmoid_gate))
    ).astype(BF16)
    up_pre = (scale * back_hidden * silu_gate).astype(BF16)
    return (scaled_hidden, gate_pre, up_pre, route_part)


LITTLE = pl.CostEstimate(flops=1, bytes_accessed=1, transcendentals=0)
LANES = 128
BLOCK = 256
OVER_LAST = (((1,), (1,)), ((), ()))


def params(mebibytes):
    return pltpu.CompilerParams(vmem_limit_bytes=mebibytes * 1024 * 1024)


def whole(shape):
    return pl.BlockSpec(shape, lambda *_: (0,) * len(shape))


def forward_kernel(n_rows, width, per_array, scalars, *refs):
    rows, (gate_ref, up_ref, down_ref, out_ref, *joined) = refs[:n_rows], refs[n_rows:]
    step = pl.program_id(0)
    rows_in = jnp.concatenate([ref[:, :width] for ref in rows], axis=0)
    rows_grad = jnp.concatenate([ref[:, width : 2 * width] for ref in rows], axis=0)
    results = (
        jnp.dot(rows_in, gate_ref[0], preferred_element_type=F32),
        jnp.dot(rows_in, up_ref[0], preferred_element_type=F32),
        lax.dot_general(rows_grad, down_ref[0], OVER_LAST, preferred_element_type=F32),
    )
    for a, result in enumerate(results):
        start = pl.multiple_of(a * per_array + step * BLOCK, BLOCK)
        out_ref[:, pl.ds(start, BLOCK)] = result.astype(BF16)
    for ref, value in zip(joined, (rows_in, rows_grad)):
        ref[...] = value


def forward_piece(scalars, rows, height, w_gate, w_up, w_down, half, per_array):
    width = w_gate.shape[1]
    steps = per_array // BLOCK
    total = height * len(rows)
    outs = [(total, 3 * per_array)] + ([(total, width)] * 2 if half == 0 else [])
    across = pl.BlockSpec((1, width, BLOCK), lambda j: (0, 0, half * steps + j))
    down = pl.BlockSpec((1, BLOCK, width), lambda j: (0, half * steps + j, 0))
    return pl.pallas_call(
        functools.partial(forward_kernel, len(rows), width, per_array),
        grid=(steps,),
        in_specs=[pl.BlockSpec(memory_space=pltpu.SMEM)]
        + [whole((height, r.shape[1])) for r in rows]
        + [across, across, down],
        out_specs=[whole(shape) for shape in outs],
        out_shape=[jax.ShapeDtypeStruct(shape, BF16) for shape in outs],
        compiler_params=params(28),
        cost_estimate=LITTLE,
    )(scalars, *rows, w_gate, w_up, w_down)


def add_kernel(a_ref, b_ref, out_ref):
    out_ref[...] = (a_ref[...].astype(F32) + b_ref[...].astype(F32)).astype(BF16)


def add_pieces(a, b):
    return pl.pallas_call(
        add_kernel,
        out_shape=jax.ShapeDtypeStruct(a.shape, BF16),
        compiler_params=params(8),
        cost_estimate=LITTLE,
    )(a, b)


def add_choose_kernel(middle_ref, a_ref, b_ref, other_ref, out_ref, both_ref):
    total = (a_ref[...].astype(F32) + b_ref[...].astype(F32)).astype(BF16)
    out_ref[...] = total
    both_ref[...] = jnp.where(middle_ref[0] == 1, total.astype(F32), other_ref[...].astype(F32)).astype(BF16)


def add_choose(middle, a, b, other):
    spec = pl.BlockSpec(memory_space=pltpu.VMEM)
    return pl.pallas_call(
        add_choose_kernel,
        in_specs=[pl.BlockSpec(memory_space=pltpu.SMEM), spec, spec, spec],
        out_specs=[spec, spec],
        out_shape=[jax.ShapeDtypeStruct(a.shape, BF16)] * 2,
        compiler_params=params(8),
        cost_estimate=LITTLE,
    )(middle, a, b, other)


def backward_kernel(n_rows, width, first, scalars, own_ref, came_ref, *refs):
    extras, refs = refs[:n_rows], refs[n_rows:]
    (gate_ref, up_ref), refs = refs[:2], refs[2:]
    if not first:
        (grad_in, route_in), refs = refs[:2], refs[5:]
    hidden_ref, gate_pre_ref, up_pre_ref = refs[:3]
    per_array = own_ref.shape[1] // 3

    def load(a):
        cols = slice(a * per_array, (a + 1) * per_array)
        return jnp.where(
            scalars[0] == 1, own_ref[:, cols].astype(F32), came_ref[:, cols].astype(F32)
        )

    tail = jnp.concatenate([ref[...] for ref in extras], axis=0).astype(F32)
    weight = jnp.where(tail[:, 2:3] == scalars[1].astype(F32), tail[:, 0:1], tail[:, 1:2])
    pre_gate, pre_up, back_hidden = load(0), load(1), load(2)
    sigmoid_gate = jax.nn.sigmoid(pre_gate)
    silu_gate = pre_gate * sigmoid_gate
    hidden = silu_gate * pre_up
    route = jnp.sum(hidden * back_hidden, axis=1, keepdims=True)
    hidden_ref[...] = (weight * hidden).astype(BF16)
    gate_pre = (
        weight * back_hidden * pre_up * sigmoid_gate * (1.0 + pre_gate * (1.0 - sigmoid_gate))
    ).astype(BF16)
    up_pre = (weight * back_hidden * silu_gate).astype(BF16)
    gate_pre_ref[...] = gate_pre
    up_pre_ref[...] = up_pre
    grad = lax.dot_general(
        gate_pre, gate_ref[0], OVER_LAST, preferred_element_type=F32
    ) + lax.dot_general(up_pre, up_ref[0], OVER_LAST, preferred_element_type=F32)
    if first:
        grad_ref, route_ref = refs[3:]
        grad_ref[...] = grad
        route_ref[...] = jnp.broadcast_to(route, route_ref.shape)
        return
    backs = refs[3:]
    grad = grad + grad_in[...]
    routes = route_in[...] + jnp.broadcast_to(route, route_in.shape)
    rows = backs[0].shape[0]
    for i, ref in enumerate(backs):
        ref[:, :width] = grad[i * rows : (i + 1) * rows, :].astype(BF16)
        ref[:, width:] = routes[i * rows : (i + 1) * rows, :].astype(BF16)


def backward_piece(scalars, own, came, rows, height, w_gate, w_up, half, before):
    width, units = w_gate.shape[1:]
    total = height * len(rows)
    per_array = own.shape[1] // 3
    across = pl.BlockSpec((1, width, per_array), lambda j: (0, 0, half))
    column = pl.BlockSpec((total, per_array), lambda j: (0, half))
    extra = pl.BlockSpec((height, LANES), lambda j: (0, 2 * width // LANES))
    sums = [(total, width), (total, LANES)]
    back = (height, width + LANES)
    in_specs = [pl.BlockSpec(memory_space=pltpu.SMEM), whole(own.shape), whole(came.shape)]
    in_specs += [extra] * len(rows) + [across, across]
    operands = [scalars, own, came, *rows, w_gate, w_up]
    aliases = {}
    if half:
        in_specs += [whole(shape) for shape in sums]
        in_specs += [pl.BlockSpec(memory_space=pl.ANY)] * 3
        operands += [*before[3:], *before[:3]]
        aliases = {len(operands) - 3 + i: i for i in range(3)}
        outs = [whole(back)] * len(rows)
        shapes = [jax.ShapeDtypeStruct(back, BF16)] * len(rows)
    else:
        outs = [whole(shape) for shape in sums]
        shapes = [jax.ShapeDtypeStruct(shape, F32) for shape in sums]
    return pl.pallas_call(
        functools.partial(backward_kernel, len(rows), width, half == 0),
        grid=(1,),
        in_specs=in_specs,
        out_specs=[column] * 3 + outs,
        out_shape=[jax.ShapeDtypeStruct((total, units), BF16)] * 3 + shapes,
        input_output_aliases=aliases,
        compiler_params=params(32),
        cost_estimate=LITTLE,
    )(*operands)


def gradient_kernel(left_ref, right_ref, before_ref, out_ref):
    added = lax.dot_general(
        left_ref[...], right_ref[...], (((0,), (0,)), ((), ())), preferred_element_type=F32
    )
    out_ref[...] = (added + before_ref[...].astype(F32)).astype(BF16)


def gradient_add(left, right, before):
    rows, height = left.shape
    wide = right.shape[1]
    block = pl.BlockSpec((BLOCK, wide), lambda j: (j, 0))
    return pl.pallas_call(
        gradient_kernel,
        grid=(height // BLOCK,),
        in_specs=[pl.BlockSpec((rows, BLOCK), lambda j: (0, j)), whole(right.shape), block],
        out_specs=block,
        out_shape=jax.ShapeDtypeStruct((height, wide), BF16),
        compiler_params=params(16),
        cost_estimate=LITTLE,
    )(left, right, before)


def tie_kernel(*refs):
    refs[-1][...] = jnp.zeros(refs[-1].shape, jnp.int32)


def tie(*arrays):
    return pl.pallas_call(
        tie_kernel,
        in_specs=[pl.BlockSpec(memory_space=pl.ANY)] * len(arrays),
        out_shape=jax.ShapeDtypeStruct((8, LANES), jnp.int32),
        cost_estimate=LITTLE,
    )(*arrays)


def body(layer_input, out_grad, routes, gate_weights, w_gate, w_up, w_down):
    groups = lax.axis_size("expert")
    n_dp = lax.axis_size("dp")
    me = lax.axis_index("expert")
    place = lax.axis_index("dp")
    tokens, width = layer_input.shape
    choose = routes.shape[1]
    capacity = 2 * tokens * choose // groups
    per_chunk = max(1, groups // 4)
    offsets = list(range(groups))
    chunks = [offsets[i : i + per_chunk] for i in range(0, groups, per_chunk)]

    partner = me ^ jnp.arange(groups, dtype=jnp.int32)
    named = routes[:, :, None] == partner[None, None, :]
    chosen = jnp.any(named, axis=1)
    rank = jnp.cumsum(chosen.astype(jnp.int32), axis=0) - 1
    rank = jnp.where(chosen, rank, -1).T
    slot = jnp.arange(capacity, dtype=jnp.int32)
    pick = (rank[:, None, :] == slot[None, :, None]).astype(BF16)

    lanes = 128
    extra = jnp.concatenate([gate_weights, routes[:, :1].astype(BF16)], axis=1)
    extra = jnp.pad(extra, ((0, 0), (0, lanes - choose - 1)))
    packed = jnp.concatenate([layer_input, out_grad, extra], axis=1)

    gate_mat, up_mat, down_mat = w_gate[0], w_up[0], w_down[0]
    over_units = (((1,), (1,)), ((), ()))
    over_rows = (((0,), (0,)), ((), ()))

    middle = (place == n_dp // 2 - 1) | (place == n_dp // 2)

    last = [None]

    def gate(*values):
        if last[0] is None:
            return values
        return lax.optimization_barrier((*values, last[0]))[:-1]

    def mark(value):
        last[0] = value
        return value

    def fetch(r):
        (one,) = gate(pick[r])
        rows = jnp.dot(one, packed, preferred_element_type=F32).astype(BF16)
        mark(rows)
        if r:
            rows = lax.ppermute(rows, "expert", [(i, i ^ r) for i in range(groups)])
        return rows

    def join(rows):
        rows = gate(*rows)
        return rows[0] if len(rows) == 1 else jnp.concatenate(rows, axis=0)

    halves = 2
    part_units = w_gate.shape[2] // halves

    def forward(rows, half):
        cols = slice(half * part_units, (half + 1) * part_units)
        rows_in, rows_grad = rows[:, :width], rows[:, width : 2 * width]
        part_gate = jnp.dot(rows_in, gate_mat[:, cols], preferred_element_type=F32)
        part_up = jnp.dot(rows_in, up_mat[:, cols], preferred_element_type=F32)
        part_back = lax.dot_general(
            rows_grad, down_mat[cols], over_units, preferred_element_type=F32
        )
        return jnp.concatenate(
            [part_gate.astype(BF16), part_up.astype(BF16), part_back.astype(BF16)], axis=1
        )

    count = len(chunks)
    pieces = halves * count
    kept = {}
    held = {}
    returned = {}

    def activate(c, sums):
        tail = held[c][:, 2 * width :]
        weight = jnp.where(tail[:, 2:3] == me.astype(BF16), tail[:, 0:1], tail[:, 1:2])
        sums = [
            jnp.concatenate([s[:, a * part_units : (a + 1) * part_units] for s in sums], axis=1)
            for a in range(3)
        ]
        scaled_hidden, gate_pre, up_pre, route_part = activation_grads(sums, weight)
        kept[c] = [
            held[c][:, :width],
            held[c][:, width : 2 * width],
            scaled_hidden,
            gate_pre,
            up_pre,
            route_part,
        ]
        mark(up_pre)

    def to_input(c):
        gate_pre, up_pre = gate(*kept[c][3:5])
        slot_grad = (
            lax.dot_general(gate_pre, gate_mat, over_units, preferred_element_type=F32)
            + lax.dot_general(up_pre, up_mat, over_units, preferred_element_type=F32)
        ).astype(BF16)
        kept[c].append(mark(slot_grad))

    def give_back(c):
        route_part, slot_grad = gate(*kept[c][5:])
        back = jnp.concatenate(
            [slot_grad, jnp.broadcast_to(route_part, (route_part.shape[0], lanes))], axis=1
        )
        for i, r in enumerate(chunks[c]):
            one = back[i * capacity : (i + 1) * capacity]
            mark(one)
            if r:
                one = lax.ppermute(one, "expert", [(i, i ^ r) for i in range(groups)])
            returned[r] = one

    combined = [None]
    route_cols = {}

    gradients = {}
    counted = {}

    def add_gradient(which):
        first = counted.get(which, 0)
        counted[which] = len(kept)
        left, right = ((2, 1), (0, 3), (0, 4))[which]
        these = [kept[c] for c in range(first, counted[which])]
        rows_left = jnp.concatenate([one[left] for one in these], axis=0)
        rows_right = jnp.concatenate([one[right] for one in these], axis=0)
        (rows_left,) = gate(rows_left)
        if first:
            gradients[which] = gradient_add(rows_left, rows_right, gradients[which])
            mark(gradients[which])
            return
        added = lax.dot_general(rows_left, rows_right, over_rows, preferred_element_type=F32)
        gradients[which] = added.astype(BF16)
        if counted[which] < count:
            gradients[which] = mark(gradients[which])

    def take_back(chunk):
        came = gate(*[returned[r] for r in chunk])
        for r, one in zip(chunk, came):
            route_cols[r] = one[:, width]
        stacked = jnp.concatenate([one[:, :width] for one in came], axis=0)
        spread = jnp.concatenate([pick[r] for r in chunk], axis=0)
        added = lax.dot_general(spread, stacked, over_rows, preferred_element_type=F32)
        if combined[0] is not None:
            added = combined[0] + added
        combined[0] = mark(added)

    if n_dp != 4:
        for c in range(count):
            held[c] = join([fetch(r) for r in chunks[c]])
            activate(c, [line_sum(forward(held[c], a), "dp", n_dp, place) for a in range(halves)])
            to_input(c)
            give_back(c)
    else:
        inward, across, outward = [(0, 1), (3, 2)], [(1, 2), (2, 1)], [(1, 0), (2, 3)]
        part, partly, total, spread_out = {}, {}, {}, {}
        arrived, crossed, joined = {}, {}, {}
        scalars = jnp.stack([middle.astype(jnp.int32), me.astype(jnp.int32)])
        pairs = {}

        ready_pairs = {}

        def pick_pair(c):
            r = chunks[c][0]
            (both,) = gate(pick[r : r + 2].reshape(2 * capacity, tokens))
            ready_pairs[c] = mark(jnp.dot(both, packed, preferred_element_type=F32).astype(BF16))

        def fetch_pair(c):
            r = chunks[c][0]
            if c not in ready_pairs:
                pick_pair(c)
            (sent,) = gate(ready_pairs[c])
            pairs[c] = lax.ppermute(sent, "expert", [(i, i ^ r) for i in range(groups)])

        others = {}

        def split(c):
            (pairs[c],) = gate(pairs[c])
            others[c] = mark(pairs[c][capacity:])

        def hand_on(c):
            (other,) = gate(others[c])
            rows[c] = [
                pairs[c],
                lax.ppermute(other, "expert", [(i, i ^ 1) for i in range(groups)]),
            ]

        rows = {}
        fetch_pair(1)
        fetch_pair(2)
        from_core = fetch(1)
        rows[0] = [fetch(0), from_core]

        def compute_part(k):
            c, half = divmod(k, halves)
            if half == 0:
                held[c] = gate(*rows[c])
            (ready,) = gate(scalars)
            part[k], *wide = forward_piece(
                ready, held[c], capacity, w_gate, w_up, w_down, half, part_units
            )
            mark(part[k])
            if half == 0:
                joined[c] = wide

        begun = {}

        def finish(k):
            c, half = divmod(k, halves)
            (came,) = gate(spread_out[k])
            results = backward_piece(
                scalars, total[k], came, held[c], capacity, w_gate, w_up, half, begun.get(c)
            )
            mark(results[3])
            if half == 0:
                begun[c] = results
                return
            kept[c] = [*joined[c], *results[:3]]
            for r, one in zip(chunks[c], results[3:]):
                if r:
                    one = lax.ppermute(one, "expert", [(i, i ^ r) for i in range(groups)])
                returned[r] = one

        work = {
            1: [(fetch_pair, 3)],
            4: [(finish, 0)],
            5: [(finish, 1)],
            6: [(finish, 2)],
            7: [(finish, 3), (take_back, chunks[0])],
            8: [(finish, 4)],
            9: [(finish, 5), (add_gradient, 0), (take_back, chunks[1])],
        }
        compute_part(0)
        arrived[0] = lax.ppermute(part[0], "dp", inward)
        compute_part(1)
        arrived[1] = lax.ppermute(part[1], "dp", inward)
        pick_pair(3)
        for t in range(1, pieces + 2):
            if t <= pieces:
                (came,) = gate(arrived[t - 1])
                partly[t - 1] = mark(add_pieces(part[t - 1], came))
                crossed[t - 1] = lax.ppermute(partly[t - 1], "dp", across)
            for c in {1: (1, 2), 4: (3,)}.get(t, ()):
                split(c)
            if t in (1, 2, 4):
                hand_on({1: 1, 2: 2, 4: 3}[t])
            if t + 1 < pieces:
                compute_part(t + 1)
            if t == 1:
                arrived[2] = lax.ppermute(part[2], "dp", inward)
            else:
                k = t - 2
                (came,) = gate(crossed[k])
                if t + 1 < pieces:
                    total[k], both = add_choose(scalars, partly[k], came, part[t + 1])
                    mark(both)
                    arrived[t + 1] = lax.ppermute(both, "dp", inward + outward)
                    spread_out[k] = arrived[t + 1]
                else:
                    total[k] = mark(add_pieces(partly[k], came))
                    spread_out[k] = lax.ppermute(total[k], "dp", outward)
            for step, c in work.get(t, ()):
                step(c)
        finish(6)
        add_gradient(1)
        add_gradient(2)
        finish(7)
        take_back(chunks[2])
    for which in range(3):
        add_gradient(which)
    grad_down, grad_gate, grad_up = (gradients[which] for which in range(3))
    mark(tie(grad_down, grad_gate, grad_up))
    if len(chunks[-1]) == 2:
        take_back(chunks[-1])
    else:
        take_back([r for r in offsets if r not in route_cols])
    input_grad = combined[0].astype(BF16)
    route_cols = jnp.stack([route_cols[r] for r in range(groups)], axis=0)
    per_offset = jnp.einsum("rst,rs->tr", pick, route_cols, preferred_element_type=F32)
    route_grad = jnp.sum(jnp.where(named, per_offset[:, None, :], 0.0), axis=2).astype(BF16)
    return (
        input_grad,
        route_grad,
        grad_gate[None],
        grad_up[None],
        grad_down[None],
    )


def solution(mesh):
    placed = (
        P("expert", "dp"),
        P("expert", "dp"),
        P("expert", None),
        P("expert", None),
        P("expert", "dp", None),
        P("expert", "dp", None),
        P("expert", None, "dp"),
    )
    return jax.shard_map(
        body,
        mesh=mesh,
        in_specs=placed,
        out_specs=(
            P("expert", "dp"),
            P("expert", None),
            P("expert", "dp", None),
            P("expert", "dp", None),
            P("expert", None, "dp"),
        ),
        check_vma=False,
    )
```

```python
import functools

import jax
import jax.numpy as jnp
from jax import lax
from jax.experimental import pallas as pl
from jax.experimental.pallas import tpu as pltpu
from jax.sharding import PartitionSpec as P

BF16 = jnp.bfloat16
F32 = jnp.float32


def line_sum(part, axis, size, place):
    half = size // 2
    total = part
    for k in range(half - 1):
        pairs = [(k, k + 1), (size - 1 - k, size - 2 - k)]
        arrived = lax.ppermute(total, axis, pairs)
        total = (total.astype(F32) + arrived.astype(F32)).astype(BF16)
    arrived = lax.ppermute(total, axis, [(half - 1, half), (half, half - 1)])
    total = (total.astype(F32) + arrived.astype(F32)).astype(BF16)
    depth = jnp.where(place < half, half - 1 - place, place - half)
    for k in range(half - 1):
        pairs = [(half - 1 - k, half - 2 - k), (half + k, half + k + 1)]
        arrived = lax.ppermute(total, axis, pairs)
        total = jnp.where(depth == k + 1, arrived, total)
    return total


def activation_grads(sums, weight):
    pre_gate, pre_up, back_hidden = (one.astype(F32) for one in sums)
    sigmoid_gate = jax.nn.sigmoid(pre_gate)
    silu_gate = pre_gate * sigmoid_gate
    hidden = silu_gate * pre_up
    route_part = jnp.sum(hidden * back_hidden, axis=1, keepdims=True).astype(BF16)
    scale = weight.astype(F32)
    scaled_hidden = (scale * hidden).astype(BF16)
    gate_pre = (
        scale * back_hidden * pre_up * sigmoid_gate * (1.0 + pre_gate * (1.0 - sigmoid_gate))
    ).astype(BF16)
    up_pre = (scale * back_hidden * silu_gate).astype(BF16)
    return (scaled_hidden, gate_pre, up_pre, route_part)


LITTLE = pl.CostEstimate(flops=1, bytes_accessed=1, transcendentals=0)
LANES = 128
BLOCK = 256
OVER_LAST = (((1,), (1,)), ((), ()))


def params(mebibytes):
    return pltpu.CompilerParams(vmem_limit_bytes=mebibytes * 1024 * 1024)


def whole(shape):
    return pl.BlockSpec(shape, lambda *_: (0,) * len(shape))


def forward_kernel(n_rows, width, per_array, scalars, *refs):
    rows, (gate_ref, up_ref, down_ref, out_ref, *joined) = refs[:n_rows], refs[n_rows:]
    step = pl.program_id(0)
    rows_in = jnp.concatenate([ref[:, :width] for ref in rows], axis=0)
    rows_grad = jnp.concatenate([ref[:, width : 2 * width] for ref in rows], axis=0)
    results = (
        jnp.dot(rows_in, gate_ref[0], preferred_element_type=F32),
        jnp.dot(rows_in, up_ref[0], preferred_element_type=F32),
        lax.dot_general(rows_grad, down_ref[0], OVER_LAST, preferred_element_type=F32),
    )
    for a, result in enumerate(results):
        start = pl.multiple_of(a * per_array + step * BLOCK, BLOCK)
        out_ref[:, pl.ds(start, BLOCK)] = result.astype(BF16)
    for ref, value in zip(joined, (rows_in, rows_grad)):
        ref[...] = value


def forward_piece(scalars, rows, height, w_gate, w_up, w_down, half, per_array):
    width = w_gate.shape[1]
    steps = per_array // BLOCK
    total = height * len(rows)
    outs = [(total, 3 * per_array)] + ([(total, width)] * 2 if half == 0 else [])
    across = pl.BlockSpec((1, width, BLOCK), lambda j: (0, 0, half * steps + j))
    down = pl.BlockSpec((1, BLOCK, width), lambda j: (0, half * steps + j, 0))
    return pl.pallas_call(
        functools.partial(forward_kernel, len(rows), width, per_array),
        grid=(steps,),
        in_specs=[pl.BlockSpec(memory_space=pltpu.SMEM)]
        + [whole((height, r.shape[1])) for r in rows]
        + [across, across, down],
        out_specs=[whole(shape) for shape in outs],
        out_shape=[jax.ShapeDtypeStruct(shape, BF16) for shape in outs],
        compiler_params=params(28),
        cost_estimate=LITTLE,
    )(scalars, *rows, w_gate, w_up, w_down)


def add_kernel(a_ref, b_ref, out_ref):
    out_ref[...] = (a_ref[...].astype(F32) + b_ref[...].astype(F32)).astype(BF16)


def add_pieces(a, b):
    return pl.pallas_call(
        add_kernel,
        out_shape=jax.ShapeDtypeStruct(a.shape, BF16),
        compiler_params=params(8),
        cost_estimate=LITTLE,
    )(a, b)


def add_choose_kernel(middle_ref, a_ref, b_ref, other_ref, out_ref, both_ref):
    total = (a_ref[...].astype(F32) + b_ref[...].astype(F32)).astype(BF16)
    out_ref[...] = total
    both_ref[...] = jnp.where(middle_ref[0] == 1, total.astype(F32), other_ref[...].astype(F32)).astype(BF16)


def add_choose(middle, a, b, other):
    spec = pl.BlockSpec(memory_space=pltpu.VMEM)
    return pl.pallas_call(
        add_choose_kernel,
        in_specs=[pl.BlockSpec(memory_space=pltpu.SMEM), spec, spec, spec],
        out_specs=[spec, spec],
        out_shape=[jax.ShapeDtypeStruct(a.shape, BF16)] * 2,
        compiler_params=params(8),
        cost_estimate=LITTLE,
    )(middle, a, b, other)


def backward_kernel(n_rows, width, first, scalars, own_ref, came_ref, *refs):
    extras, refs = refs[:n_rows], refs[n_rows:]
    (gate_ref, up_ref), refs = refs[:2], refs[2:]
    if not first:
        (grad_in, route_in), refs = refs[:2], refs[5:]
    hidden_ref, gate_pre_ref, up_pre_ref = refs[:3]
    per_array = own_ref.shape[1] // 3

    def load(a):
        cols = slice(a * per_array, (a + 1) * per_array)
        return jnp.where(
            scalars[0] == 1, own_ref[:, cols].astype(F32), came_ref[:, cols].astype(F32)
        )

    tail = jnp.concatenate([ref[...] for ref in extras], axis=0).astype(F32)
    weight = jnp.where(tail[:, 2:3] == scalars[1].astype(F32), tail[:, 0:1], tail[:, 1:2])
    pre_gate, pre_up, back_hidden = load(0), load(1), load(2)
    sigmoid_gate = jax.nn.sigmoid(pre_gate)
    silu_gate = pre_gate * sigmoid_gate
    hidden = silu_gate * pre_up
    route = jnp.sum(hidden * back_hidden, axis=1, keepdims=True)
    hidden_ref[...] = (weight * hidden).astype(BF16)
    gate_pre = (
        weight * back_hidden * pre_up * sigmoid_gate * (1.0 + pre_gate * (1.0 - sigmoid_gate))
    ).astype(BF16)
    up_pre = (weight * back_hidden * silu_gate).astype(BF16)
    gate_pre_ref[...] = gate_pre
    up_pre_ref[...] = up_pre
    grad = lax.dot_general(
        gate_pre, gate_ref[0], OVER_LAST, preferred_element_type=F32
    ) + lax.dot_general(up_pre, up_ref[0], OVER_LAST, preferred_element_type=F32)
    if first:
        grad_ref, route_ref = refs[3:]
        grad_ref[...] = grad
        route_ref[...] = jnp.broadcast_to(route, route_ref.shape)
        return
    backs = refs[3:]
    grad = grad + grad_in[...]
    routes = route_in[...] + jnp.broadcast_to(route, route_in.shape)
    rows = backs[0].shape[0]
    for i, ref in enumerate(backs):
        ref[:, :width] = grad[i * rows : (i + 1) * rows, :].astype(BF16)
        ref[:, width:] = routes[i * rows : (i + 1) * rows, :].astype(BF16)


def backward_piece(scalars, own, came, rows, height, w_gate, w_up, half, before):
    width, units = w_gate.shape[1:]
    total = height * len(rows)
    per_array = own.shape[1] // 3
    across = pl.BlockSpec((1, width, per_array), lambda j: (0, 0, half))
    column = pl.BlockSpec((total, per_array), lambda j: (0, half))
    extra = pl.BlockSpec((height, LANES), lambda j: (0, 2 * width // LANES))
    sums = [(total, width), (total, LANES)]
    back = (height, width + LANES)
    in_specs = [pl.BlockSpec(memory_space=pltpu.SMEM), whole(own.shape), whole(came.shape)]
    in_specs += [extra] * len(rows) + [across, across]
    operands = [scalars, own, came, *rows, w_gate, w_up]
    aliases = {}
    if half:
        in_specs += [whole(shape) for shape in sums]
        in_specs += [pl.BlockSpec(memory_space=pl.ANY)] * 3
        operands += [*before[3:], *before[:3]]
        aliases = {len(operands) - 3 + i: i for i in range(3)}
        outs = [whole(back)] * len(rows)
        shapes = [jax.ShapeDtypeStruct(back, BF16)] * len(rows)
    else:
        outs = [whole(shape) for shape in sums]
        shapes = [jax.ShapeDtypeStruct(shape, F32) for shape in sums]
    return pl.pallas_call(
        functools.partial(backward_kernel, len(rows), width, half == 0),
        grid=(1,),
        in_specs=in_specs,
        out_specs=[column] * 3 + outs,
        out_shape=[jax.ShapeDtypeStruct((total, units), BF16)] * 3 + shapes,
        input_output_aliases=aliases,
        compiler_params=params(32),
        cost_estimate=LITTLE,
    )(*operands)


def gradient_kernel(left_ref, right_ref, before_ref, out_ref):
    added = lax.dot_general(
        left_ref[...], right_ref[...], (((0,), (0,)), ((), ())), preferred_element_type=F32
    )
    out_ref[...] = (added + before_ref[...].astype(F32)).astype(BF16)


def gradient_add(left, right, before):
    rows, height = left.shape
    wide = right.shape[1]
    block = pl.BlockSpec((BLOCK, wide), lambda j: (j, 0))
    return pl.pallas_call(
        gradient_kernel,
        grid=(height // BLOCK,),
        in_specs=[pl.BlockSpec((rows, BLOCK), lambda j: (0, j)), whole(right.shape), block],
        out_specs=block,
        out_shape=jax.ShapeDtypeStruct((height, wide), BF16),
        compiler_params=params(16),
        cost_estimate=LITTLE,
    )(left, right, before)


def tie_kernel(*refs):
    refs[-1][...] = jnp.zeros(refs[-1].shape, jnp.int32)


def tie(*arrays):
    return pl.pallas_call(
        tie_kernel,
        in_specs=[pl.BlockSpec(memory_space=pl.ANY)] * len(arrays),
        out_shape=jax.ShapeDtypeStruct((8, LANES), jnp.int32),
        cost_estimate=LITTLE,
    )(*arrays)


def body(layer_input, out_grad, routes, gate_weights, w_gate, w_up, w_down):
    groups = lax.axis_size("expert")
    n_dp = lax.axis_size("dp")
    me = lax.axis_index("expert")
    place = lax.axis_index("dp")
    tokens, width = layer_input.shape
    choose = routes.shape[1]
    capacity = 2 * tokens * choose // groups
    per_chunk = max(1, groups // 4)
    offsets = list(range(groups))
    chunks = [offsets[i : i + per_chunk] for i in range(0, groups, per_chunk)]

    partner = me ^ jnp.arange(groups, dtype=jnp.int32)
    named = routes[:, :, None] == partner[None, None, :]
    chosen = jnp.any(named, axis=1)
    rank = jnp.cumsum(chosen.astype(jnp.int32), axis=0) - 1
    rank = jnp.where(chosen, rank, -1).T
    slot = jnp.arange(capacity, dtype=jnp.int32)
    pick = (rank[:, None, :] == slot[None, :, None]).astype(BF16)

    lanes = 128
    extra = jnp.concatenate([gate_weights, routes[:, :1].astype(BF16)], axis=1)
    extra = jnp.pad(extra, ((0, 0), (0, lanes - choose - 1)))
    packed = jnp.concatenate([layer_input, out_grad, extra], axis=1)

    gate_mat, up_mat, down_mat = w_gate[0], w_up[0], w_down[0]
    over_units = (((1,), (1,)), ((), ()))
    over_rows = (((0,), (0,)), ((), ()))

    middle = (place == n_dp // 2 - 1) | (place == n_dp // 2)

    last = [None]

    def gate(*values):
        if last[0] is None:
            return values
        return lax.optimization_barrier((*values, last[0]))[:-1]

    def mark(value):
        last[0] = value
        return value

    def fetch(r):
        (one,) = gate(pick[r])
        rows = jnp.dot(one, packed, preferred_element_type=F32).astype(BF16)
        mark(rows)
        if r:
            rows = lax.ppermute(rows, "expert", [(i, i ^ r) for i in range(groups)])
        return rows

    def join(rows):
        rows = gate(*rows)
        return rows[0] if len(rows) == 1 else jnp.concatenate(rows, axis=0)

    halves = 2
    part_units = w_gate.shape[2] // halves

    def forward(rows, half):
        cols = slice(half * part_units, (half + 1) * part_units)
        rows_in, rows_grad = rows[:, :width], rows[:, width : 2 * width]
        part_gate = jnp.dot(rows_in, gate_mat[:, cols], preferred_element_type=F32)
        part_up = jnp.dot(rows_in, up_mat[:, cols], preferred_element_type=F32)
        part_back = lax.dot_general(
            rows_grad, down_mat[cols], over_units, preferred_element_type=F32
        )
        return jnp.concatenate(
            [part_gate.astype(BF16), part_up.astype(BF16), part_back.astype(BF16)], axis=1
        )

    count = len(chunks)
    pieces = halves * count
    kept = {}
    held = {}
    returned = {}

    def activate(c, sums):
        tail = held[c][:, 2 * width :]
        weight = jnp.where(tail[:, 2:3] == me.astype(BF16), tail[:, 0:1], tail[:, 1:2])
        sums = [
            jnp.concatenate([s[:, a * part_units : (a + 1) * part_units] for s in sums], axis=1)
            for a in range(3)
        ]
        scaled_hidden, gate_pre, up_pre, route_part = activation_grads(sums, weight)
        kept[c] = [
            held[c][:, :width],
            held[c][:, width : 2 * width],
            scaled_hidden,
            gate_pre,
            up_pre,
            route_part,
        ]
        mark(up_pre)

    def to_input(c):
        gate_pre, up_pre = gate(*kept[c][3:5])
        slot_grad = (
            lax.dot_general(gate_pre, gate_mat, over_units, preferred_element_type=F32)
            + lax.dot_general(up_pre, up_mat, over_units, preferred_element_type=F32)
        ).astype(BF16)
        kept[c].append(mark(slot_grad))

    def give_back(c):
        route_part, slot_grad = gate(*kept[c][5:])
        back = jnp.concatenate(
            [slot_grad, jnp.broadcast_to(route_part, (route_part.shape[0], lanes))], axis=1
        )
        for i, r in enumerate(chunks[c]):
            one = back[i * capacity : (i + 1) * capacity]
            mark(one)
            if r:
                one = lax.ppermute(one, "expert", [(i, i ^ r) for i in range(groups)])
            returned[r] = one

    combined = [None]
    route_cols = {}

    gradients = {}
    counted = {}

    def add_gradient(which):
        first = counted.get(which, 0)
        counted[which] = len(kept)
        left, right = ((2, 1), (0, 3), (0, 4))[which]
        these = [kept[c] for c in range(first, counted[which])]
        rows_left = jnp.concatenate([one[left] for one in these], axis=0)
        rows_right = jnp.concatenate([one[right] for one in these], axis=0)
        (rows_left,) = gate(rows_left)
        if first:
            gradients[which] = gradient_add(rows_left, rows_right, gradients[which])
            mark(gradients[which])
            return
        added = lax.dot_general(rows_left, rows_right, over_rows, preferred_element_type=F32)
        gradients[which] = added.astype(BF16)
        if counted[which] < count:
            gradients[which] = mark(gradients[which])

    def take_back(chunk):
        came = gate(*[returned[r] for r in chunk])
        for r, one in zip(chunk, came):
            route_cols[r] = one[:, width]
        stacked = jnp.concatenate([one[:, :width] for one in came], axis=0)
        spread = jnp.concatenate([pick[r] for r in chunk], axis=0)
        added = lax.dot_general(spread, stacked, over_rows, preferred_element_type=F32)
        if combined[0] is not None:
            added = combined[0] + added
        combined[0] = mark(added)

    if n_dp != 4:
        for c in range(count):
            held[c] = join([fetch(r) for r in chunks[c]])
            activate(c, [line_sum(forward(held[c], a), "dp", n_dp, place) for a in range(halves)])
            to_input(c)
            give_back(c)
    else:
        inward, across, outward = [(0, 1), (3, 2)], [(1, 2), (2, 1)], [(1, 0), (2, 3)]
        part, partly, total, spread_out = {}, {}, {}, {}
        arrived, crossed, joined = {}, {}, {}
        scalars = jnp.stack([middle.astype(jnp.int32), me.astype(jnp.int32)])
        pairs = {}

        ready_pairs = {}

        def pick_pair(c):
            r = chunks[c][0]
            (both,) = gate(pick[r : r + 2].reshape(2 * capacity, tokens))
            ready_pairs[c] = mark(jnp.dot(both, packed, preferred_element_type=F32).astype(BF16))

        def fetch_pair(c):
            r = chunks[c][0]
            if c not in ready_pairs:
                pick_pair(c)
            (sent,) = gate(ready_pairs[c])
            pairs[c] = lax.ppermute(sent, "expert", [(i, i ^ r) for i in range(groups)])

        others = {}

        def split(c):
            (pairs[c],) = gate(pairs[c])
            others[c] = mark(pairs[c][capacity:])

        def hand_on(c):
            (other,) = gate(others[c])
            rows[c] = [
                pairs[c],
                lax.ppermute(other, "expert", [(i, i ^ 1) for i in range(groups)]),
            ]

        rows = {}
        fetch_pair(1)
        fetch_pair(2)
        from_core = fetch(1)
        rows[0] = [fetch(0), from_core]

        def compute_part(k):
            c, half = divmod(k, halves)
            if half == 0:
                held[c] = gate(*rows[c])
            (ready,) = gate(scalars)
            part[k], *wide = forward_piece(
                ready, held[c], capacity, w_gate, w_up, w_down, half, part_units
            )
            mark(part[k])
            if half == 0:
                joined[c] = wide

        begun = {}

        def finish(k):
            c, half = divmod(k, halves)
            (came,) = gate(spread_out[k])
            results = backward_piece(
                scalars, total[k], came, held[c], capacity, w_gate, w_up, half, begun.get(c)
            )
            mark(results[3])
            if half == 0:
                begun[c] = results
                return
            kept[c] = [*joined[c], *results[:3]]
            for r, one in zip(chunks[c], results[3:]):
                if r:
                    one = lax.ppermute(one, "expert", [(i, i ^ r) for i in range(groups)])
                returned[r] = one

        work = {
            1: [(fetch_pair, 3)],
            4: [(finish, 0)],
            5: [(finish, 1)],
            6: [(finish, 2)],
            7: [(finish, 3), (take_back, chunks[0])],
            8: [(finish, 4), (finish, 5), (add_gradient, 0)],
            9: [(take_back, chunks[1]), (add_gradient, 1), (add_gradient, 2)],
        }
        compute_part(0)
        arrived[0] = lax.ppermute(part[0], "dp", inward)
        compute_part(1)
        arrived[1] = lax.ppermute(part[1], "dp", inward)
        pick_pair(3)
        for t in range(1, pieces + 2):
            if t <= pieces:
                (came,) = gate(arrived[t - 1])
                partly[t - 1] = mark(add_pieces(part[t - 1], came))
                crossed[t - 1] = lax.ppermute(partly[t - 1], "dp", across)
            for c in {1: (1, 2), 4: (3,)}.get(t, ()):
                split(c)
            if t in (1, 2, 4):
                hand_on({1: 1, 2: 2, 4: 3}[t])
            if t + 1 < pieces:
                compute_part(t + 1)
            if t == 1:
                arrived[2] = lax.ppermute(part[2], "dp", inward)
            else:
                k = t - 2
                (came,) = gate(crossed[k])
                if t + 1 < pieces:
                    total[k], both = add_choose(scalars, partly[k], came, part[t + 1])
                    mark(both)
                    arrived[t + 1] = lax.ppermute(both, "dp", inward + outward)
                    spread_out[k] = arrived[t + 1]
                else:
                    total[k] = mark(add_pieces(partly[k], came))
                    spread_out[k] = lax.ppermute(total[k], "dp", outward)
            for step, c in work.get(t, ()):
                step(c)
        finish(6)
        finish(7)
        take_back(chunks[2])
    for which in range(3):
        add_gradient(which)
    grad_down, grad_gate, grad_up = (gradients[which] for which in range(3))
    mark(tie(grad_down, grad_gate, grad_up))
    if len(chunks[-1]) == 2:
        take_back(chunks[-1])
    else:
        take_back([r for r in offsets if r not in route_cols])
    input_grad = combined[0].astype(BF16)
    route_cols = jnp.stack([route_cols[r] for r in range(groups)], axis=0)
    per_offset = jnp.einsum("rst,rs->tr", pick, route_cols, preferred_element_type=F32)
    route_grad = jnp.sum(jnp.where(named, per_offset[:, None, :], 0.0), axis=2).astype(BF16)
    return (
        input_grad,
        route_grad,
        grad_gate[None],
        grad_up[None],
        grad_down[None],
    )


def solution(mesh):
    placed = (
        P("expert", "dp"),
        P("expert", "dp"),
        P("expert", None),
        P("expert", None),
        P("expert", "dp", None),
        P("expert", "dp", None),
        P("expert", None, "dp"),
    )
    return jax.shard_map(
        body,
        mesh=mesh,
        in_specs=placed,
        out_specs=(
            P("expert", "dp"),
            P("expert", None),
            P("expert", "dp", None),
            P("expert", "dp", None),
            P("expert", None, "dp"),
        ),
        check_vma=False,
    )
```

```python
import functools

import jax
import jax.numpy as jnp
from jax import lax
from jax.experimental import pallas as pl
from jax.experimental.pallas import tpu as pltpu
from jax.sharding import PartitionSpec as P

BF16 = jnp.bfloat16
F32 = jnp.float32


def line_sum(part, axis, size, place):
    half = size // 2
    total = part
    for k in range(half - 1):
        pairs = [(k, k + 1), (size - 1 - k, size - 2 - k)]
        arrived = lax.ppermute(total, axis, pairs)
        total = (total.astype(F32) + arrived.astype(F32)).astype(BF16)
    arrived = lax.ppermute(total, axis, [(half - 1, half), (half, half - 1)])
    total = (total.astype(F32) + arrived.astype(F32)).astype(BF16)
    depth = jnp.where(place < half, half - 1 - place, place - half)
    for k in range(half - 1):
        pairs = [(half - 1 - k, half - 2 - k), (half + k, half + k + 1)]
        arrived = lax.ppermute(total, axis, pairs)
        total = jnp.where(depth == k + 1, arrived, total)
    return total


def activation_grads(sums, weight):
    pre_gate, pre_up, back_hidden = (one.astype(F32) for one in sums)
    sigmoid_gate = jax.nn.sigmoid(pre_gate)
    silu_gate = pre_gate * sigmoid_gate
    hidden = silu_gate * pre_up
    route_part = jnp.sum(hidden * back_hidden, axis=1, keepdims=True).astype(BF16)
    scale = weight.astype(F32)
    scaled_hidden = (scale * hidden).astype(BF16)
    gate_pre = (
        scale * back_hidden * pre_up * sigmoid_gate * (1.0 + pre_gate * (1.0 - sigmoid_gate))
    ).astype(BF16)
    up_pre = (scale * back_hidden * silu_gate).astype(BF16)
    return (scaled_hidden, gate_pre, up_pre, route_part)


LITTLE = pl.CostEstimate(flops=1, bytes_accessed=1, transcendentals=0)
LANES = 128
BLOCK = 256
OVER_LAST = (((1,), (1,)), ((), ()))


def params(mebibytes):
    return pltpu.CompilerParams(vmem_limit_bytes=mebibytes * 1024 * 1024)


def whole(shape):
    return pl.BlockSpec(shape, lambda *_: (0,) * len(shape))


def forward_kernel(n_rows, width, per_array, scalars, *refs):
    rows, (gate_ref, up_ref, down_ref, out_ref, *joined) = refs[:n_rows], refs[n_rows:]
    step = pl.program_id(0)
    rows_in = jnp.concatenate([ref[:, :width] for ref in rows], axis=0)
    rows_grad = jnp.concatenate([ref[:, width : 2 * width] for ref in rows], axis=0)
    results = (
        jnp.dot(rows_in, gate_ref[0], preferred_element_type=F32),
        jnp.dot(rows_in, up_ref[0], preferred_element_type=F32),
        lax.dot_general(rows_grad, down_ref[0], OVER_LAST, preferred_element_type=F32),
    )
    for a, result in enumerate(results):
        start = pl.multiple_of(a * per_array + step * BLOCK, BLOCK)
        out_ref[:, pl.ds(start, BLOCK)] = result.astype(BF16)
    for ref, value in zip(joined, (rows_in, rows_grad)):
        ref[...] = value


def forward_piece(scalars, rows, height, w_gate, w_up, w_down, half, per_array):
    width = w_gate.shape[1]
    steps = per_array // BLOCK
    total = height * len(rows)
    outs = [(total, 3 * per_array)] + ([(total, width)] * 2 if half == 0 else [])
    across = pl.BlockSpec((1, width, BLOCK), lambda j: (0, 0, half * steps + j))
    down = pl.BlockSpec((1, BLOCK, width), lambda j: (0, half * steps + j, 0))
    return pl.pallas_call(
        functools.partial(forward_kernel, len(rows), width, per_array),
        grid=(steps,),
        in_specs=[pl.BlockSpec(memory_space=pltpu.SMEM)]
        + [whole((height, r.shape[1])) for r in rows]
        + [across, across, down],
        out_specs=[whole(shape) for shape in outs],
        out_shape=[jax.ShapeDtypeStruct(shape, BF16) for shape in outs],
        compiler_params=params(28),
        cost_estimate=LITTLE,
    )(scalars, *rows, w_gate, w_up, w_down)


def add_kernel(a_ref, b_ref, out_ref):
    out_ref[...] = (a_ref[...].astype(F32) + b_ref[...].astype(F32)).astype(BF16)


def add_pieces(a, b):
    return pl.pallas_call(
        add_kernel,
        out_shape=jax.ShapeDtypeStruct(a.shape, BF16),
        compiler_params=params(8),
        cost_estimate=LITTLE,
    )(a, b)


def add_choose_kernel(middle_ref, a_ref, b_ref, other_ref, out_ref, both_ref):
    total = (a_ref[...].astype(F32) + b_ref[...].astype(F32)).astype(BF16)
    out_ref[...] = total
    both_ref[...] = jnp.where(middle_ref[0] == 1, total.astype(F32), other_ref[...].astype(F32)).astype(BF16)


def add_choose(middle, a, b, other):
    spec = pl.BlockSpec(memory_space=pltpu.VMEM)
    return pl.pallas_call(
        add_choose_kernel,
        in_specs=[pl.BlockSpec(memory_space=pltpu.SMEM), spec, spec, spec],
        out_specs=[spec, spec],
        out_shape=[jax.ShapeDtypeStruct(a.shape, BF16)] * 2,
        compiler_params=params(8),
        cost_estimate=LITTLE,
    )(middle, a, b, other)


def backward_kernel(n_rows, width, first, scalars, own_ref, came_ref, *refs):
    extras, refs = refs[:n_rows], refs[n_rows:]
    (gate_ref, up_ref), refs = refs[:2], refs[2:]
    if not first:
        (grad_in, route_in), refs = refs[:2], refs[5:]
    hidden_ref, gate_pre_ref, up_pre_ref = refs[:3]
    per_array = own_ref.shape[1] // 3

    def load(a):
        cols = slice(a * per_array, (a + 1) * per_array)
        return jnp.where(
            scalars[0] == 1, own_ref[:, cols].astype(F32), came_ref[:, cols].astype(F32)
        )

    tail = jnp.concatenate([ref[...] for ref in extras], axis=0).astype(F32)
    weight = jnp.where(tail[:, 2:3] == scalars[1].astype(F32), tail[:, 0:1], tail[:, 1:2])
    pre_gate, pre_up, back_hidden = load(0), load(1), load(2)
    sigmoid_gate = jax.nn.sigmoid(pre_gate)
    silu_gate = pre_gate * sigmoid_gate
    hidden = silu_gate * pre_up
    route = jnp.sum(hidden * back_hidden, axis=1, keepdims=True)
    hidden_ref[...] = (weight * hidden).astype(BF16)
    gate_pre = (
        weight * back_hidden * pre_up * sigmoid_gate * (1.0 + pre_gate * (1.0 - sigmoid_gate))
    ).astype(BF16)
    up_pre = (weight * back_hidden * silu_gate).astype(BF16)
    gate_pre_ref[...] = gate_pre
    up_pre_ref[...] = up_pre
    grad = lax.dot_general(
        gate_pre, gate_ref[0], OVER_LAST, preferred_element_type=F32
    ) + lax.dot_general(up_pre, up_ref[0], OVER_LAST, preferred_element_type=F32)
    if first:
        grad_ref, route_ref = refs[3:]
        grad_ref[...] = grad
        route_ref[...] = jnp.broadcast_to(route, route_ref.shape)
        return
    backs = refs[3:]
    grad = grad + grad_in[...]
    routes = route_in[...] + jnp.broadcast_to(route, route_in.shape)
    rows = backs[0].shape[0]
    for i, ref in enumerate(backs):
        ref[:, :width] = grad[i * rows : (i + 1) * rows, :].astype(BF16)
        ref[:, width:] = routes[i * rows : (i + 1) * rows, :].astype(BF16)


def backward_piece(scalars, own, came, rows, height, w_gate, w_up, half, before):
    width, units = w_gate.shape[1:]
    total = height * len(rows)
    per_array = own.shape[1] // 3
    across = pl.BlockSpec((1, width, per_array), lambda j: (0, 0, half))
    column = pl.BlockSpec((total, per_array), lambda j: (0, half))
    extra = pl.BlockSpec((height, LANES), lambda j: (0, 2 * width // LANES))
    sums = [(total, width), (total, LANES)]
    back = (height, width + LANES)
    in_specs = [pl.BlockSpec(memory_space=pltpu.SMEM), whole(own.shape), whole(came.shape)]
    in_specs += [extra] * len(rows) + [across, across]
    operands = [scalars, own, came, *rows, w_gate, w_up]
    aliases = {}
    if half:
        in_specs += [whole(shape) for shape in sums]
        in_specs += [pl.BlockSpec(memory_space=pl.ANY)] * 3
        operands += [*before[3:], *before[:3]]
        aliases = {len(operands) - 3 + i: i for i in range(3)}
        outs = [whole(back)] * len(rows)
        shapes = [jax.ShapeDtypeStruct(back, BF16)] * len(rows)
    else:
        outs = [whole(shape) for shape in sums]
        shapes = [jax.ShapeDtypeStruct(shape, F32) for shape in sums]
    return pl.pallas_call(
        functools.partial(backward_kernel, len(rows), width, half == 0),
        grid=(1,),
        in_specs=in_specs,
        out_specs=[column] * 3 + outs,
        out_shape=[jax.ShapeDtypeStruct((total, units), BF16)] * 3 + shapes,
        input_output_aliases=aliases,
        compiler_params=params(32),
        cost_estimate=LITTLE,
    )(*operands)


def gradient_kernel(left_ref, right_ref, before_ref, out_ref):
    added = lax.dot_general(
        left_ref[...], right_ref[...], (((0,), (0,)), ((), ())), preferred_element_type=F32
    )
    out_ref[...] = (added + before_ref[...].astype(F32)).astype(BF16)


def gradient_add(left, right, before):
    rows, height = left.shape
    wide = right.shape[1]
    block = pl.BlockSpec((BLOCK, wide), lambda j: (j, 0))
    return pl.pallas_call(
        gradient_kernel,
        grid=(height // BLOCK,),
        in_specs=[pl.BlockSpec((rows, BLOCK), lambda j: (0, j)), whole(right.shape), block],
        out_specs=block,
        out_shape=jax.ShapeDtypeStruct((height, wide), BF16),
        compiler_params=params(16),
        cost_estimate=LITTLE,
    )(left, right, before)


def tie_kernel(*refs):
    refs[-1][...] = jnp.zeros(refs[-1].shape, jnp.int32)


def tie(*arrays):
    return pl.pallas_call(
        tie_kernel,
        in_specs=[pl.BlockSpec(memory_space=pl.ANY)] * len(arrays),
        out_shape=jax.ShapeDtypeStruct((8, LANES), jnp.int32),
        cost_estimate=LITTLE,
    )(*arrays)


def body(layer_input, out_grad, routes, gate_weights, w_gate, w_up, w_down):
    groups = lax.axis_size("expert")
    n_dp = lax.axis_size("dp")
    me = lax.axis_index("expert")
    place = lax.axis_index("dp")
    tokens, width = layer_input.shape
    choose = routes.shape[1]
    capacity = 2 * tokens * choose // groups
    per_chunk = max(1, groups // 4)
    offsets = list(range(groups))
    chunks = [offsets[i : i + per_chunk] for i in range(0, groups, per_chunk)]

    partner = me ^ jnp.arange(groups, dtype=jnp.int32)
    named = routes[:, :, None] == partner[None, None, :]
    chosen = jnp.any(named, axis=1)
    rank = jnp.cumsum(chosen.astype(jnp.int32), axis=0) - 1
    rank = jnp.where(chosen, rank, -1).T
    slot = jnp.arange(capacity, dtype=jnp.int32)
    pick = (rank[:, None, :] == slot[None, :, None]).astype(BF16)

    lanes = 128
    extra = jnp.concatenate([gate_weights, routes[:, :1].astype(BF16)], axis=1)
    extra = jnp.pad(extra, ((0, 0), (0, lanes - choose - 1)))
    packed = jnp.concatenate([layer_input, out_grad, extra], axis=1)

    gate_mat, up_mat, down_mat = w_gate[0], w_up[0], w_down[0]
    over_units = (((1,), (1,)), ((), ()))
    over_rows = (((0,), (0,)), ((), ()))

    middle = (place == n_dp // 2 - 1) | (place == n_dp // 2)

    last = [None]

    def gate(*values):
        if last[0] is None:
            return values
        return lax.optimization_barrier((*values, last[0]))[:-1]

    def mark(value):
        last[0] = value
        return value

    def fetch(r):
        (one,) = gate(pick[r])
        rows = jnp.dot(one, packed, preferred_element_type=F32).astype(BF16)
        mark(rows)
        if r:
            rows = lax.ppermute(rows, "expert", [(i, i ^ r) for i in range(groups)])
        return rows

    def join(rows):
        rows = gate(*rows)
        return rows[0] if len(rows) == 1 else jnp.concatenate(rows, axis=0)

    halves = 2
    part_units = w_gate.shape[2] // halves

    def forward(rows, half):
        cols = slice(half * part_units, (half + 1) * part_units)
        rows_in, rows_grad = rows[:, :width], rows[:, width : 2 * width]
        part_gate = jnp.dot(rows_in, gate_mat[:, cols], preferred_element_type=F32)
        part_up = jnp.dot(rows_in, up_mat[:, cols], preferred_element_type=F32)
        part_back = lax.dot_general(
            rows_grad, down_mat[cols], over_units, preferred_element_type=F32
        )
        return jnp.concatenate(
            [part_gate.astype(BF16), part_up.astype(BF16), part_back.astype(BF16)], axis=1
        )

    count = len(chunks)
    pieces = halves * count
    kept = {}
    held = {}
    returned = {}

    def activate(c, sums):
        tail = held[c][:, 2 * width :]
        weight = jnp.where(tail[:, 2:3] == me.astype(BF16), tail[:, 0:1], tail[:, 1:2])
        sums = [
            jnp.concatenate([s[:, a * part_units : (a + 1) * part_units] for s in sums], axis=1)
            for a in range(3)
        ]
        scaled_hidden, gate_pre, up_pre, route_part = activation_grads(sums, weight)
        kept[c] = [
            held[c][:, :width],
            held[c][:, width : 2 * width],
            scaled_hidden,
            gate_pre,
            up_pre,
            route_part,
        ]
        mark(up_pre)

    def to_input(c):
        gate_pre, up_pre = gate(*kept[c][3:5])
        slot_grad = (
            lax.dot_general(gate_pre, gate_mat, over_units, preferred_element_type=F32)
            + lax.dot_general(up_pre, up_mat, over_units, preferred_element_type=F32)
        ).astype(BF16)
        kept[c].append(mark(slot_grad))

    def give_back(c):
        route_part, slot_grad = gate(*kept[c][5:])
        back = jnp.concatenate(
            [slot_grad, jnp.broadcast_to(route_part, (route_part.shape[0], lanes))], axis=1
        )
        for i, r in enumerate(chunks[c]):
            one = back[i * capacity : (i + 1) * capacity]
            mark(one)
            if r:
                one = lax.ppermute(one, "expert", [(i, i ^ r) for i in range(groups)])
            returned[r] = one

    combined = [None]
    route_cols = {}

    gradients = {}
    counted = {}

    def add_gradient(which):
        first = counted.get(which, 0)
        counted[which] = len(kept)
        left, right = ((2, 1), (0, 3), (0, 4))[which]
        these = [kept[c] for c in range(first, counted[which])]
        rows_left = jnp.concatenate([one[left] for one in these], axis=0)
        rows_right = jnp.concatenate([one[right] for one in these], axis=0)
        (rows_left,) = gate(rows_left)
        if first:
            gradients[which] = gradient_add(rows_left, rows_right, gradients[which])
            mark(gradients[which])
            return
        added = lax.dot_general(rows_left, rows_right, over_rows, preferred_element_type=F32)
        gradients[which] = added.astype(BF16)
        if counted[which] < count:
            gradients[which] = mark(gradients[which])

    def take_back(chunk):
        came = gate(*[returned[r] for r in chunk])
        for r, one in zip(chunk, came):
            route_cols[r] = one[:, width]
        stacked = jnp.concatenate([one[:, :width] for one in came], axis=0)
        spread = jnp.concatenate([pick[r] for r in chunk], axis=0)
        added = lax.dot_general(spread, stacked, over_rows, preferred_element_type=F32)
        if combined[0] is not None:
            added = combined[0] + added
        combined[0] = mark(added)

    if n_dp != 4:
        for c in range(count):
            held[c] = join([fetch(r) for r in chunks[c]])
            activate(c, [line_sum(forward(held[c], a), "dp", n_dp, place) for a in range(halves)])
            to_input(c)
            give_back(c)
    else:
        inward, across, outward = [(0, 1), (3, 2)], [(1, 2), (2, 1)], [(1, 0), (2, 3)]
        part, partly, total, spread_out = {}, {}, {}, {}
        arrived, crossed, joined = {}, {}, {}
        scalars = jnp.stack([middle.astype(jnp.int32), me.astype(jnp.int32)])
        pairs = {}

        ready_pairs = {}

        def pick_pair(c):
            r = chunks[c][0]
            (both,) = gate(pick[r : r + 2].reshape(2 * capacity, tokens))
            ready_pairs[c] = mark(jnp.dot(both, packed, preferred_element_type=F32).astype(BF16))

        def fetch_pair(c):
            r = chunks[c][0]
            if c not in ready_pairs:
                pick_pair(c)
            (sent,) = gate(ready_pairs[c])
            pairs[c] = lax.ppermute(sent, "expert", [(i, i ^ r) for i in range(groups)])

        others = {}

        def split(c):
            (pairs[c],) = gate(pairs[c])
            others[c] = mark(pairs[c][capacity:])

        def hand_on(c):
            (other,) = gate(others[c])
            rows[c] = [
                pairs[c],
                lax.ppermute(other, "expert", [(i, i ^ 1) for i in range(groups)]),
            ]

        rows = {}
        fetch_pair(1)
        fetch_pair(2)
        from_core = fetch(1)
        rows[0] = [fetch(0), from_core]

        def compute_part(k):
            c, half = divmod(k, halves)
            if half == 0:
                held[c] = gate(*rows[c])
            (ready,) = gate(scalars)
            part[k], *wide = forward_piece(
                ready, held[c], capacity, w_gate, w_up, w_down, half, part_units
            )
            mark(part[k])
            if half == 0:
                joined[c] = wide

        begun = {}

        def finish(k):
            c, half = divmod(k, halves)
            (came,) = gate(spread_out[k])
            results = backward_piece(
                scalars, total[k], came, held[c], capacity, w_gate, w_up, half, begun.get(c)
            )
            mark(results[3])
            if half == 0:
                begun[c] = results
                return
            kept[c] = [*joined[c], *results[:3]]
            for r, one in zip(chunks[c], results[3:]):
                if r:
                    one = lax.ppermute(one, "expert", [(i, i ^ r) for i in range(groups)])
                returned[r] = one

        work = {
            1: [(fetch_pair, 3)],
            4: [(finish, 0)],
            5: [(finish, 1)],
            6: [(finish, 2)],
            7: [(finish, 3), (take_back, chunks[0])],
            8: [(finish, 4), (finish, 5)],
            9: [(take_back, chunks[1]), (add_gradient, 0), (add_gradient, 1), (add_gradient, 2)],
        }
        compute_part(0)
        arrived[0] = lax.ppermute(part[0], "dp", inward)
        compute_part(1)
        arrived[1] = lax.ppermute(part[1], "dp", inward)
        pick_pair(3)
        for t in range(1, pieces + 2):
            if t <= pieces:
                (came,) = gate(arrived[t - 1])
                partly[t - 1] = mark(add_pieces(part[t - 1], came))
                crossed[t - 1] = lax.ppermute(partly[t - 1], "dp", across)
            for c in {1: (1, 2), 4: (3,)}.get(t, ()):
                split(c)
            if t in (1, 2, 4):
                hand_on({1: 1, 2: 2, 4: 3}[t])
            if t + 1 < pieces:
                compute_part(t + 1)
            if t == 1:
                arrived[2] = lax.ppermute(part[2], "dp", inward)
            else:
                k = t - 2
                (came,) = gate(crossed[k])
                if t + 1 < pieces:
                    total[k], both = add_choose(scalars, partly[k], came, part[t + 1])
                    mark(both)
                    arrived[t + 1] = lax.ppermute(both, "dp", inward + outward)
                    spread_out[k] = arrived[t + 1]
                else:
                    total[k] = mark(add_pieces(partly[k], came))
                    spread_out[k] = lax.ppermute(total[k], "dp", outward)
            for step, c in work.get(t, ()):
                step(c)
        finish(6)
        finish(7)
        take_back(chunks[2])
    for which in range(3):
        add_gradient(which)
    grad_down, grad_gate, grad_up = (gradients[which] for which in range(3))
    mark(tie(grad_down, grad_gate, grad_up))
    if len(chunks[-1]) == 2:
        take_back(chunks[-1])
    else:
        take_back([r for r in offsets if r not in route_cols])
    input_grad = combined[0].astype(BF16)
    route_cols = jnp.stack([route_cols[r] for r in range(groups)], axis=0)
    per_offset = jnp.einsum("rst,rs->tr", pick, route_cols, preferred_element_type=F32)
    route_grad = jnp.sum(jnp.where(named, per_offset[:, None, :], 0.0), axis=2).astype(BF16)
    return (
        input_grad,
        route_grad,
        grad_gate[None],
        grad_up[None],
        grad_down[None],
    )


def solution(mesh):
    placed = (
        P("expert", "dp"),
        P("expert", "dp"),
        P("expert", None),
        P("expert", None),
        P("expert", "dp", None),
        P("expert", "dp", None),
        P("expert", None, "dp"),
    )
    return jax.shard_map(
        body,
        mesh=mesh,
        in_specs=placed,
        out_specs=(
            P("expert", "dp"),
            P("expert", None),
            P("expert", "dp", None),
            P("expert", "dp", None),
            P("expert", None, "dp"),
        ),
        check_vma=False,
    )
```

```python
import functools

import jax
import jax.numpy as jnp
from jax import lax
from jax.experimental import pallas as pl
from jax.experimental.pallas import tpu as pltpu
from jax.sharding import PartitionSpec as P

BF16 = jnp.bfloat16
F32 = jnp.float32


def line_sum(part, axis, size, place):
    half = size // 2
    total = part
    for k in range(half - 1):
        pairs = [(k, k + 1), (size - 1 - k, size - 2 - k)]
        arrived = lax.ppermute(total, axis, pairs)
        total = (total.astype(F32) + arrived.astype(F32)).astype(BF16)
    arrived = lax.ppermute(total, axis, [(half - 1, half), (half, half - 1)])
    total = (total.astype(F32) + arrived.astype(F32)).astype(BF16)
    depth = jnp.where(place < half, half - 1 - place, place - half)
    for k in range(half - 1):
        pairs = [(half - 1 - k, half - 2 - k), (half + k, half + k + 1)]
        arrived = lax.ppermute(total, axis, pairs)
        total = jnp.where(depth == k + 1, arrived, total)
    return total


def activation_grads(sums, weight):
    pre_gate, pre_up, back_hidden = (one.astype(F32) for one in sums)
    sigmoid_gate = jax.nn.sigmoid(pre_gate)
    silu_gate = pre_gate * sigmoid_gate
    hidden = silu_gate * pre_up
    route_part = jnp.sum(hidden * back_hidden, axis=1, keepdims=True).astype(BF16)
    scale = weight.astype(F32)
    scaled_hidden = (scale * hidden).astype(BF16)
    gate_pre = (
        scale * back_hidden * pre_up * sigmoid_gate * (1.0 + pre_gate * (1.0 - sigmoid_gate))
    ).astype(BF16)
    up_pre = (scale * back_hidden * silu_gate).astype(BF16)
    return (scaled_hidden, gate_pre, up_pre, route_part)


LITTLE = pl.CostEstimate(flops=1, bytes_accessed=1, transcendentals=0)
LANES = 128
BLOCK = 256
OVER_LAST = (((1,), (1,)), ((), ()))


def params(mebibytes):
    return pltpu.CompilerParams(vmem_limit_bytes=mebibytes * 1024 * 1024)


def whole(shape):
    return pl.BlockSpec(shape, lambda *_: (0,) * len(shape))


def forward_kernel(n_rows, width, per_array, scalars, *refs):
    rows, (gate_ref, up_ref, down_ref, out_ref, *joined) = refs[:n_rows], refs[n_rows:]
    step = pl.program_id(0)
    rows_in = jnp.concatenate([ref[:, :width] for ref in rows], axis=0)
    rows_grad = jnp.concatenate([ref[:, width : 2 * width] for ref in rows], axis=0)
    results = (
        jnp.dot(rows_in, gate_ref[0], preferred_element_type=F32),
        jnp.dot(rows_in, up_ref[0], preferred_element_type=F32),
        lax.dot_general(rows_grad, down_ref[0], OVER_LAST, preferred_element_type=F32),
    )
    for a, result in enumerate(results):
        start = pl.multiple_of(a * per_array + step * BLOCK, BLOCK)
        out_ref[:, pl.ds(start, BLOCK)] = result.astype(BF16)
    for ref, value in zip(joined, (rows_in, rows_grad)):
        ref[...] = value


def forward_piece(scalars, rows, height, w_gate, w_up, w_down, half, per_array):
    width = w_gate.shape[1]
    steps = per_array // BLOCK
    total = height * len(rows)
    outs = [(total, 3 * per_array)] + ([(total, width)] * 2 if half == 0 else [])
    across = pl.BlockSpec((1, width, BLOCK), lambda j: (0, 0, half * steps + j))
    down = pl.BlockSpec((1, BLOCK, width), lambda j: (0, half * steps + j, 0))
    return pl.pallas_call(
        functools.partial(forward_kernel, len(rows), width, per_array),
        grid=(steps,),
        in_specs=[pl.BlockSpec(memory_space=pltpu.SMEM)]
        + [whole((height, r.shape[1])) for r in rows]
        + [across, across, down],
        out_specs=[whole(shape) for shape in outs],
        out_shape=[jax.ShapeDtypeStruct(shape, BF16) for shape in outs],
        compiler_params=params(28),
        cost_estimate=LITTLE,
    )(scalars, *rows, w_gate, w_up, w_down)


def add_kernel(a_ref, b_ref, out_ref):
    out_ref[...] = (a_ref[...].astype(F32) + b_ref[...].astype(F32)).astype(BF16)


def add_pieces(a, b):
    return pl.pallas_call(
        add_kernel,
        out_shape=jax.ShapeDtypeStruct(a.shape, BF16),
        compiler_params=params(8),
        cost_estimate=LITTLE,
    )(a, b)


def add_choose_kernel(middle_ref, a_ref, b_ref, other_ref, out_ref, both_ref):
    total = (a_ref[...].astype(F32) + b_ref[...].astype(F32)).astype(BF16)
    out_ref[...] = total
    both_ref[...] = jnp.where(middle_ref[0] == 1, total.astype(F32), other_ref[...].astype(F32)).astype(BF16)


def add_choose(middle, a, b, other):
    spec = pl.BlockSpec(memory_space=pltpu.VMEM)
    return pl.pallas_call(
        add_choose_kernel,
        in_specs=[pl.BlockSpec(memory_space=pltpu.SMEM), spec, spec, spec],
        out_specs=[spec, spec],
        out_shape=[jax.ShapeDtypeStruct(a.shape, BF16)] * 2,
        compiler_params=params(8),
        cost_estimate=LITTLE,
    )(middle, a, b, other)


def backward_kernel(n_rows, width, first, scalars, own_ref, came_ref, *refs):
    extras, refs = refs[:n_rows], refs[n_rows:]
    (gate_ref, up_ref), refs = refs[:2], refs[2:]
    if not first:
        (grad_in, route_in), refs = refs[:2], refs[5:]
    hidden_ref, gate_pre_ref, up_pre_ref = refs[:3]
    per_array = own_ref.shape[1] // 3

    def load(a):
        cols = slice(a * per_array, (a + 1) * per_array)
        return jnp.where(
            scalars[0] == 1, own_ref[:, cols].astype(F32), came_ref[:, cols].astype(F32)
        )

    tail = jnp.concatenate([ref[...] for ref in extras], axis=0).astype(F32)
    weight = jnp.where(tail[:, 2:3] == scalars[1].astype(F32), tail[:, 0:1], tail[:, 1:2])
    pre_gate, pre_up, back_hidden = load(0), load(1), load(2)
    sigmoid_gate = jax.nn.sigmoid(pre_gate)
    silu_gate = pre_gate * sigmoid_gate
    hidden = silu_gate * pre_up
    route = jnp.sum(hidden * back_hidden, axis=1, keepdims=True)
    hidden_ref[...] = (weight * hidden).astype(BF16)
    gate_pre = (
        weight * back_hidden * pre_up * sigmoid_gate * (1.0 + pre_gate * (1.0 - sigmoid_gate))
    ).astype(BF16)
    up_pre = (weight * back_hidden * silu_gate).astype(BF16)
    gate_pre_ref[...] = gate_pre
    up_pre_ref[...] = up_pre
    grad = lax.dot_general(
        gate_pre, gate_ref[0], OVER_LAST, preferred_element_type=F32
    ) + lax.dot_general(up_pre, up_ref[0], OVER_LAST, preferred_element_type=F32)
    if first:
        grad_ref, route_ref = refs[3:]
        grad_ref[...] = grad
        route_ref[...] = jnp.broadcast_to(route, route_ref.shape)
        return
    backs = refs[3:]
    grad = grad + grad_in[...]
    routes = route_in[...] + jnp.broadcast_to(route, route_in.shape)
    rows = backs[0].shape[0]
    for i, ref in enumerate(backs):
        ref[:, :width] = grad[i * rows : (i + 1) * rows, :].astype(BF16)
        ref[:, width:] = routes[i * rows : (i + 1) * rows, :].astype(BF16)


def backward_piece(scalars, own, came, rows, height, w_gate, w_up, half, before):
    width, units = w_gate.shape[1:]
    total = height * len(rows)
    per_array = own.shape[1] // 3
    across = pl.BlockSpec((1, width, per_array), lambda j: (0, 0, half))
    column = pl.BlockSpec((total, per_array), lambda j: (0, half))
    extra = pl.BlockSpec((height, LANES), lambda j: (0, 2 * width // LANES))
    sums = [(total, width), (total, LANES)]
    back = (height, width + LANES)
    in_specs = [pl.BlockSpec(memory_space=pltpu.SMEM), whole(own.shape), whole(came.shape)]
    in_specs += [extra] * len(rows) + [across, across]
    operands = [scalars, own, came, *rows, w_gate, w_up]
    aliases = {}
    if half:
        in_specs += [whole(shape) for shape in sums]
        in_specs += [pl.BlockSpec(memory_space=pl.ANY)] * 3
        operands += [*before[3:], *before[:3]]
        aliases = {len(operands) - 3 + i: i for i in range(3)}
        outs = [whole(back)] * len(rows)
        shapes = [jax.ShapeDtypeStruct(back, BF16)] * len(rows)
    else:
        outs = [whole(shape) for shape in sums]
        shapes = [jax.ShapeDtypeStruct(shape, F32) for shape in sums]
    return pl.pallas_call(
        functools.partial(backward_kernel, len(rows), width, half == 0),
        grid=(1,),
        in_specs=in_specs,
        out_specs=[column] * 3 + outs,
        out_shape=[jax.ShapeDtypeStruct((total, units), BF16)] * 3 + shapes,
        input_output_aliases=aliases,
        compiler_params=params(32),
        cost_estimate=LITTLE,
    )(*operands)


def gradient_kernel(left_ref, right_ref, before_ref, out_ref):
    added = lax.dot_general(
        left_ref[...], right_ref[...], (((0,), (0,)), ((), ())), preferred_element_type=F32
    )
    out_ref[...] = (added + before_ref[...].astype(F32)).astype(BF16)


def gradient_add(left, right, before):
    rows, height = left.shape
    wide = right.shape[1]
    block = pl.BlockSpec((BLOCK, wide), lambda j: (j, 0))
    return pl.pallas_call(
        gradient_kernel,
        grid=(height // BLOCK,),
        in_specs=[pl.BlockSpec((rows, BLOCK), lambda j: (0, j)), whole(right.shape), block],
        out_specs=block,
        out_shape=jax.ShapeDtypeStruct((height, wide), BF16),
        compiler_params=params(16),
        cost_estimate=LITTLE,
    )(left, right, before)


def tie_kernel(*refs):
    refs[-1][...] = jnp.zeros(refs[-1].shape, jnp.int32)


def tie(*arrays):
    return pl.pallas_call(
        tie_kernel,
        in_specs=[pl.BlockSpec(memory_space=pl.ANY)] * len(arrays),
        out_shape=jax.ShapeDtypeStruct((8, LANES), jnp.int32),
        cost_estimate=LITTLE,
    )(*arrays)


def body(layer_input, out_grad, routes, gate_weights, w_gate, w_up, w_down):
    groups = lax.axis_size("expert")
    n_dp = lax.axis_size("dp")
    me = lax.axis_index("expert")
    place = lax.axis_index("dp")
    tokens, width = layer_input.shape
    choose = routes.shape[1]
    capacity = 2 * tokens * choose // groups
    per_chunk = max(1, groups // 4)
    offsets = [0, 1, 3, 5, 6, 7, 2, 4] if groups == 8 else list(range(groups))
    chunks = [offsets[i : i + per_chunk] for i in range(0, groups, per_chunk)]

    partner = me ^ jnp.arange(groups, dtype=jnp.int32)
    named = routes[:, :, None] == partner[None, None, :]
    chosen = jnp.any(named, axis=1)
    rank = jnp.cumsum(chosen.astype(jnp.int32), axis=0) - 1
    rank = jnp.where(chosen, rank, -1).T
    slot = jnp.arange(capacity, dtype=jnp.int32)
    pick = (rank[:, None, :] == slot[None, :, None]).astype(BF16)

    lanes = 128
    extra = jnp.concatenate([gate_weights, routes[:, :1].astype(BF16)], axis=1)
    extra = jnp.pad(extra, ((0, 0), (0, lanes - choose - 1)))
    packed = jnp.concatenate([layer_input, out_grad, extra], axis=1)

    gate_mat, up_mat, down_mat = w_gate[0], w_up[0], w_down[0]
    over_units = (((1,), (1,)), ((), ()))
    over_rows = (((0,), (0,)), ((), ()))

    middle = (place == n_dp // 2 - 1) | (place == n_dp // 2)

    last = [None]

    def gate(*values):
        if last[0] is None:
            return values
        return lax.optimization_barrier((*values, last[0]))[:-1]

    def mark(value):
        last[0] = value
        return value

    def fetch(r):
        (one,) = gate(pick[r])
        rows = jnp.dot(one, packed, preferred_element_type=F32).astype(BF16)
        mark(rows)
        if r:
            rows = lax.ppermute(rows, "expert", [(i, i ^ r) for i in range(groups)])
        return rows

    def join(rows):
        rows = gate(*rows)
        return rows[0] if len(rows) == 1 else jnp.concatenate(rows, axis=0)

    halves = 2
    part_units = w_gate.shape[2] // halves

    def forward(rows, half):
        cols = slice(half * part_units, (half + 1) * part_units)
        rows_in, rows_grad = rows[:, :width], rows[:, width : 2 * width]
        part_gate = jnp.dot(rows_in, gate_mat[:, cols], preferred_element_type=F32)
        part_up = jnp.dot(rows_in, up_mat[:, cols], preferred_element_type=F32)
        part_back = lax.dot_general(
            rows_grad, down_mat[cols], over_units, preferred_element_type=F32
        )
        return jnp.concatenate(
            [part_gate.astype(BF16), part_up.astype(BF16), part_back.astype(BF16)], axis=1
        )

    count = len(chunks)
    pieces = halves * count
    kept = {}
    held = {}
    returned = {}

    def activate(c, sums):
        tail = held[c][:, 2 * width :]
        weight = jnp.where(tail[:, 2:3] == me.astype(BF16), tail[:, 0:1], tail[:, 1:2])
        sums = [
            jnp.concatenate([s[:, a * part_units : (a + 1) * part_units] for s in sums], axis=1)
            for a in range(3)
        ]
        scaled_hidden, gate_pre, up_pre, route_part = activation_grads(sums, weight)
        kept[c] = [
            held[c][:, :width],
            held[c][:, width : 2 * width],
            scaled_hidden,
            gate_pre,
            up_pre,
            route_part,
        ]
        mark(up_pre)

    def to_input(c):
        gate_pre, up_pre = gate(*kept[c][3:5])
        slot_grad = (
            lax.dot_general(gate_pre, gate_mat, over_units, preferred_element_type=F32)
            + lax.dot_general(up_pre, up_mat, over_units, preferred_element_type=F32)
        ).astype(BF16)
        kept[c].append(mark(slot_grad))

    def give_back(c):
        route_part, slot_grad = gate(*kept[c][5:])
        back = jnp.concatenate(
            [slot_grad, jnp.broadcast_to(route_part, (route_part.shape[0], lanes))], axis=1
        )
        for i, r in enumerate(chunks[c]):
            one = back[i * capacity : (i + 1) * capacity]
            mark(one)
            if r:
                one = lax.ppermute(one, "expert", [(i, i ^ r) for i in range(groups)])
            returned[r] = one

    combined = [None]
    route_cols = {}

    gradients = {}
    counted = {}

    def add_gradient(which):
        first = counted.get(which, 0)
        counted[which] = len(kept)
        left, right = ((2, 1), (0, 3), (0, 4))[which]
        these = [kept[c] for c in range(first, counted[which])]
        rows_left = jnp.concatenate([one[left] for one in these], axis=0)
        rows_right = jnp.concatenate([one[right] for one in these], axis=0)
        (rows_left,) = gate(rows_left)
        if first:
            gradients[which] = gradient_add(rows_left, rows_right, gradients[which])
            mark(gradients[which])
            return
        added = lax.dot_general(rows_left, rows_right, over_rows, preferred_element_type=F32)
        gradients[which] = added.astype(BF16)
        if counted[which] < count:
            gradients[which] = mark(gradients[which])

    def take_back(chunk):
        came = gate(*[returned[r] for r in chunk])
        for r, one in zip(chunk, came):
            route_cols[r] = one[:, width]
        stacked = jnp.concatenate([one[:, :width] for one in came], axis=0)
        spread = jnp.concatenate([pick[r] for r in chunk], axis=0)
        added = lax.dot_general(spread, stacked, over_rows, preferred_element_type=F32)
        if combined[0] is not None:
            added = combined[0] + added
        combined[0] = mark(added)

    if n_dp != 4:
        for c in range(count):
            held[c] = join([fetch(r) for r in chunks[c]])
            activate(c, [line_sum(forward(held[c], a), "dp", n_dp, place) for a in range(halves)])
            to_input(c)
            give_back(c)
    else:
        inward, across, outward = [(0, 1), (3, 2)], [(1, 2), (2, 1)], [(1, 0), (2, 3)]
        part, partly, total, spread_out = {}, {}, {}, {}
        arrived, crossed, joined = {}, {}, {}
        scalars = jnp.stack([middle.astype(jnp.int32), me.astype(jnp.int32)])
        pairs = {}

        ready_pairs = {}

        def pick_pair(c):
            r = chunks[c][0]
            (both,) = gate(pick[r : r + 2].reshape(2 * capacity, tokens))
            ready_pairs[c] = mark(jnp.dot(both, packed, preferred_element_type=F32).astype(BF16))

        def fetch_pair(c):
            r = chunks[c][0]
            if c not in ready_pairs:
                pick_pair(c)
            (sent,) = gate(ready_pairs[c])
            pairs[c] = lax.ppermute(sent, "expert", [(i, i ^ r) for i in range(groups)])

        others = {}

        def split(c):
            (pairs[c],) = gate(pairs[c])
            others[c] = mark(pairs[c][capacity:])

        def hand_on(c):
            (other,) = gate(others[c])
            rows[c] = [
                pairs[c],
                lax.ppermute(other, "expert", [(i, i ^ 1) for i in range(groups)]),
            ]

        def fetch_last(c):
            rows[c] = [fetch(r) for r in chunks[c]]

        rows = {}
        from_core = fetch(1)
        rows[1] = [fetch(r) for r in chunks[1]]
        rows[0] = [fetch(0), from_core]

        def compute_part(k):
            c, half = divmod(k, halves)
            if half == 0:
                held[c] = gate(*rows[c])
            (ready,) = gate(scalars)
            part[k], *wide = forward_piece(
                ready, held[c], capacity, w_gate, w_up, w_down, half, part_units
            )
            mark(part[k])
            if half == 0:
                joined[c] = wide

        begun = {}

        def finish(k):
            c, half = divmod(k, halves)
            (came,) = gate(spread_out[k])
            results = backward_piece(
                scalars, total[k], came, held[c], capacity, w_gate, w_up, half, begun.get(c)
            )
            mark(results[3])
            if half == 0:
                begun[c] = results
                return
            kept[c] = [*joined[c], *results[:3]]
            for r, one in zip(chunks[c], results[3:]):
                if r:
                    one = lax.ppermute(one, "expert", [(i, i ^ r) for i in range(groups)])
                returned[r] = one

        work = {
            1: [(fetch_pair, 2)],
            2: [(split, 2), (hand_on, 2)],
            3: [(fetch_last, 3)],
            4: [(finish, 0)],
            5: [(finish, 1)],
            6: [(finish, 2)],
            7: [(finish, 3), (take_back, chunks[0])],
            8: [(finish, 4), (finish, 5)],
            9: [(take_back, chunks[1]), (add_gradient, 0), (add_gradient, 1), (add_gradient, 2)],
        }
        compute_part(0)
        arrived[0] = lax.ppermute(part[0], "dp", inward)
        compute_part(1)
        arrived[1] = lax.ppermute(part[1], "dp", inward)
        pick_pair(2)
        for t in range(1, pieces + 2):
            if t <= pieces:
                (came,) = gate(arrived[t - 1])
                partly[t - 1] = mark(add_pieces(part[t - 1], came))
                crossed[t - 1] = lax.ppermute(partly[t - 1], "dp", across)
            if t + 1 < pieces:
                compute_part(t + 1)
            if t == 1:
                arrived[2] = lax.ppermute(part[2], "dp", inward)
            else:
                k = t - 2
                (came,) = gate(crossed[k])
                if t + 1 < pieces:
                    total[k], both = add_choose(scalars, partly[k], came, part[t + 1])
                    mark(both)
                    arrived[t + 1] = lax.ppermute(both, "dp", inward + outward)
                    spread_out[k] = arrived[t + 1]
                else:
                    total[k] = mark(add_pieces(partly[k], came))
                    spread_out[k] = lax.ppermute(total[k], "dp", outward)
            for step, c in work.get(t, ()):
                step(c)
        finish(6)
        finish(7)
        take_back(chunks[2])
    for which in range(3):
        add_gradient(which)
    grad_down, grad_gate, grad_up = (gradients[which] for which in range(3))
    mark(tie(grad_down, grad_gate, grad_up))
    if len(chunks[-1]) == 2:
        take_back(chunks[-1])
    else:
        take_back([r for r in offsets if r not in route_cols])
    input_grad = combined[0].astype(BF16)
    route_cols = jnp.stack([route_cols[r] for r in range(groups)], axis=0)
    per_offset = jnp.einsum("rst,rs->tr", pick, route_cols, preferred_element_type=F32)
    route_grad = jnp.sum(jnp.where(named, per_offset[:, None, :], 0.0), axis=2).astype(BF16)
    return (
        input_grad,
        route_grad,
        grad_gate[None],
        grad_up[None],
        grad_down[None],
    )


def solution(mesh):
    placed = (
        P("expert", "dp"),
        P("expert", "dp"),
        P("expert", None),
        P("expert", None),
        P("expert", "dp", None),
        P("expert", "dp", None),
        P("expert", None, "dp"),
    )
    return jax.shard_map(
        body,
        mesh=mesh,
        in_specs=placed,
        out_specs=(
            P("expert", "dp"),
            P("expert", None),
            P("expert", "dp", None),
            P("expert", "dp", None),
            P("expert", None, "dp"),
        ),
        check_vma=False,
    )
```
